256 devices in a mesh: expert: 8 (over y, core), fsdp: 32 (over x, z).
Axes of the slice: x: 4, y: 4, z: 8, core: 2. Of those that a mesh axis runs over, the one named last changes fastest.
Arguments:
- tokens: bfloat16 [32768, 3072], P(('expert', 'fsdp')), may hold values from -6 to 6
- cotangent: bfloat16 [32768, 3072], P(('expert', 'fsdp')), may hold values from -6 to 6
- expert_ids: int32 [32768, 2], P(('expert', 'fsdp')), may hold values from 0 to 7, all different within a row; in each aligned block of 128 rows (0 to 127, 128 to 255, ...) at most 40 rows name the same one
- probs: bfloat16 [32768, 2], P(('expert', 'fsdp')), may hold values from 0.049804688 to 0.94921875
- gate_tiles: bfloat16 [8, 32, 128, 128], P('expert', 'fsdp'), may hold values from -0.5 to 0.5
- up_tiles: bfloat16 [8, 32, 128, 128], P('expert', 'fsdp'), may hold values from -0.5 to 0.5
- down_tiles: bfloat16 [8, 32, 128, 128], P('expert', 'fsdp'), may hold values from -0.5 to 0.5
- in_ids: int32 [8, 32], P('expert'), may hold values from 0 to 1535, as said below
- in_count: int32 [8, 32], P('expert'), may hold values from 0 to 1, as said below
- out_ids: int32 [8, 32], P('expert'), may hold values from 0 to 23
- out_count: int32 [8, 32], P('expert'), may hold values from 0 to 1, as said below
Outputs:
- token_grad: bfloat16 [32768, 3072], P(('expert', 'fsdp'))
- prob_grad: bfloat16 [32768, 2], P(('expert', 'fsdp'))
- gate_grad: float32 [8, 32, 128, 128], P('expert', 'fsdp')
- up_grad: float32 [8, 32, 128, 128], P('expert', 'fsdp')
- down_grad: float32 [8, 32, 128, 128], P('expert', 'fsdp')
The draws below stay inside these ranges and needn't reach their ends.
Inputs may be any that keep to these rules, and one draw needn't show every extreme that they name: `expert_ids`: in each block of the rows of one device no expert is named more than 40 times. The column blocks in_ids % (64) of the 32 entries of one expert differ from one another. `in_count`: some device of each expert has all its slots live. `out_count`: some device of each expert has all its slots live.
All inputs are finite; a program needn't handle non-finite values.
Results may differ from the reference program's by a relative error of at most 0.0052.
Values may be sent and summed in bfloat16 or wider, within the bound.
No kernel may reach another device: no remote copies, remote signals or barrier semaphores. Data moves between devices by JAX's collectives and lax.ppermute only.
A program may use at most 128 MiB of HBM per device.

```python
import math
import jax
import jax.numpy as jnp
import numpy as np
from jax import lax

D = 3072
FF = 8192
TOP = 2
TILE = 128
TILES_DEV = 1
TOK_DEV = 128
EXPERTS = 8
CAP = 40
TOKENS = 32768
SLOTS = 32
N_EXPERT = 8
N_FSDP = 32
DEVICES = 256


def tile_counts(key):
    first, second = jax.random.split(key)
    counts = jax.random.randint(first, (EXPERTS, N_FSDP), 0, TILES_DEV + 1)
    fullest = jax.random.randint(second, (EXPERTS, 1), 0, N_FSDP)
    return jnp.where(jnp.arange(N_FSDP)[None, :] == fullest, TILES_DEV, counts).astype(jnp.int32)


def draw_in_ids(key, part):
    key = jax.random.fold_in(key, 3)
    first, second = jax.random.split(key)
    col_blocks = FF // TILE
    keys = jax.random.split(first, EXPERTS)
    columns = jax.vmap(lambda single: jax.random.permutation(single, col_blocks)[:SLOTS])(keys)
    rows_drawn = jax.random.randint(second, (EXPERTS, SLOTS), 0, D // TILE)
    return (rows_drawn * col_blocks + columns).astype(jnp.int32)


def draw_in_count(key, part):
    key = jax.random.fold_in(key, 5)
    return tile_counts(key)


def draw_out_ids(key, part):
    key = jax.random.fold_in(key, 7)
    return jax.random.randint(key, (EXPERTS, SLOTS), 0, D // TILE).astype(jnp.int32)


def draw_out_count(key, part):
    key = jax.random.fold_in(key, 9)
    return tile_counts(key)


def block_scale(own_key, extent, pieces, smallest, largest):
    def one(axis_at, blocks):
        heights = jax.random.uniform(jax.random.fold_in(jax.random.fold_in(own_key, 6), axis_at), (blocks,), jnp.float32, smallest / len(pieces), largest / len(pieces))
        return jnp.repeat(jnp.exp(heights), extent[axis_at] // blocks).reshape((-1,) + (1,) * (len(extent) - axis_at - 1))

    factor_of = one(*pieces[0])
    for cut in pieces[1:]:
        factor_of = factor_of * one(*cut)
    return factor_of


def deal_out(stream_key, own, number, rows, count, top, limit, slope):
    ranking = jax.random.permutation(stream_key, count)
    packed, common = portions_of(count, rows * top, limit, slope, True), portions_of(count, rows * top, limit, slope, False)
    places = jnp.arange(count)

    def named(sizes, turn):
        used = int((sizes > 0).sum())
        fixed = max(1, used // 4)
        shifted = fixed + (places - fixed + turn * (used - fixed)) % max(1, count - fixed)
        return jnp.zeros((count,), jnp.int32).at[ranking[jnp.where(places < fixed, places, shifted)]].set(jnp.asarray(sizes, jnp.int32))

    sizes = jnp.where(number % 4 == 0, named(packed, number // 4), named(common, number - number // 4 - 1))
    mixed = jax.random.permutation(jax.random.fold_in(own, 3), count)
    source_of, sink = mixed[0:count // 2 * 2:2], mixed[1:count // 2 * 2:2]
    slack = jnp.minimum(sizes[source_of] - 1, limit - sizes[sink]) // 2
    slack = jnp.where((source_of == ranking[0]) | (sink == ranking[0]) | (sizes[sink] == 0), 0, jnp.maximum(slack, 0))
    shifted = jax.random.randint(jax.random.fold_in(own, 4), (count // 2,), 0, 1 << 20) % (slack + 1)
    sizes = sizes.at[source_of].add(-shifted).at[sink].add(shifted)
    members = jnp.searchsorted(jnp.cumsum(sizes), jnp.arange(rows * top), side="right").astype(jnp.int32)
    table = members.reshape(top, rows).T
    table = table[jax.random.permutation(jax.random.fold_in(own, 1), rows)]
    turn = jax.random.randint(jax.random.fold_in(own, 2), (rows, 1), 0, top)
    return jnp.take_along_axis(table, (jnp.arange(top)[None, :] + turn) % top, axis=1)


def portions_of(count, total, bound, lean, full):
    loads = [(1 << 20) // math.isqrt(grade ** lean) + 1 for grade in range(1, count + 1)]
    largest = bound if full else min(bound, max(-(-total // count), total * loads[0] // sum(loads)))
    least = 1 if total - largest >= count - 1 else 0
    given, spare = [largest] + [least] * (count - 1), total - largest - least * (count - 1)
    while spare > 0:
        movable = [i for i in range(1, count) if given[i] < largest] or [i for i in range(1, count) if given[i] < bound]
        pool, left = sum([loads[i] for i in movable]), spare
        for i in movable:
            addition = min(bound - given[i], max(1, left * loads[i] // pool), spare)
            given[i] = given[i] + addition
            spare = spare - addition
    return np.array(given)


def centred(key, extent, width, reach, pieces=(), kind=jnp.bfloat16):
    result = jax.random.normal(key, extent, jnp.float32) * width
    if len(pieces) > 0:
        result = block_scale(key, extent, pieces, -0.22, 0.18) * result
    return jnp.clip(result, min=-reach, max=reach).astype(kind)


def setup_inputs(seed: int = 0) -> dict:
    streams_of = jax.random.split(jax.random.key(seed), 12)
    tokens = centred(streams_of[0], (TOKENS, D), 1.0, 6.0, ((0, 256),))
    cotangent = centred(streams_of[1], (TOKENS, D), 0.5, 6.0, ((0, 256),))
    expert_ids_keys = jax.random.split(jax.random.fold_in(streams_of[2], 1), TOKENS // TOK_DEV)
    expert_ids_turns = jax.random.permutation(jax.random.fold_in(streams_of[2], 3), TOKENS // TOK_DEV)
    expert_ids = jax.vmap(lambda own, number: deal_out(jax.random.fold_in(streams_of[2], 2), own, number, TOK_DEV, EXPERTS, TOP, CAP, 2))(expert_ids_keys, expert_ids_turns).reshape((TOKENS, TOP))
    probs = jnp.clip(0.049804688 + 0.89941406 * jax.random.uniform(streams_of[3], (TOKENS, TOP), jnp.float32) ** block_scale(streams_of[3], (TOKENS, TOP), ((0, 256),), -0.2, 0.2), 0.049804688, 0.94921875).astype(jnp.bfloat16)
    gate_tiles = centred(streams_of[4], (EXPERTS, SLOTS, TILE, TILE), TILE ** -0.5, 0.5, ((0, 8), (1, 32)))
    up_tiles = centred(streams_of[5], (EXPERTS, SLOTS, TILE, TILE), TILE ** -0.5, 0.5, ((0, 8), (1, 32)))
    down_tiles = centred(streams_of[6], (EXPERTS, SLOTS, TILE, TILE), TILE ** -0.5, 0.5, ((0, 8), (1, 32)))
    in_ids = draw_in_ids(jax.random.fold_in(streams_of[11], 71), 0)
    in_count = draw_in_count(jax.random.fold_in(streams_of[11], 71), 0)
    out_ids = draw_out_ids(jax.random.fold_in(streams_of[11], 71), 0)
    out_count = draw_out_count(jax.random.fold_in(streams_of[11], 71), 0)
    return {"tokens": tokens, "cotangent": cotangent, "expert_ids": expert_ids, "probs": probs, "gate_tiles": gate_tiles, "up_tiles": up_tiles, "down_tiles": down_tiles, "in_ids": in_ids, "in_count": in_count, "out_ids": out_ids, "out_count": out_count}


def slot_positions(block_ids, capacity):
    flat = block_ids.reshape(-1).astype(jnp.int32)
    onehot = (flat[:, None] == jnp.arange(EXPERTS, dtype=jnp.int32)[None, :]).astype(jnp.int32)
    before = jnp.cumsum(onehot, axis=0) - onehot
    return (flat * capacity + jnp.sum(before * onehot, axis=1)).astype(jnp.int32)


def place_terms(terms, index_to, blocks):
    return jnp.zeros((blocks,) + terms.shape[1:], jnp.float32).at[index_to].add(terms)


def live_slots(counts):
    return (jnp.arange(TILES_DEV, dtype=jnp.int32)[None, :] < counts[:, None]).reshape(-1)


def expert_rows(x_t, dy_t, p_rows, gate, up, down, in_ids, out_ids, live_in, live_out):
    row_blocks = x_t.shape[0]
    col_blocks = FF // TILE
    in_row = (in_ids // col_blocks).astype(jnp.int32)
    in_col = (in_ids % col_blocks).astype(jnp.int32)
    out_row = in_col
    out_col = out_ids.astype(jnp.int32)
    gate32 = gate.astype(jnp.float32)
    up32 = up.astype(jnp.float32)
    down32 = down.astype(jnp.float32)
    x_sel = jnp.take(x_t, in_row, axis=0).astype(jnp.float32)
    g = place_terms(jnp.einsum("sri,sij->srj", x_sel, gate32), in_col, col_blocks)
    u = place_terms(jnp.einsum("sri,sij->srj", x_sel, up32), in_col, col_blocks)
    sig = jax.nn.sigmoid(g)
    act = g * sig
    hidden = (act * u).astype(jnp.bfloat16)
    dy_sel = jnp.take(dy_t, out_col, axis=0).astype(jnp.float32)
    m = place_terms(jnp.einsum("srj,sij->sri", dy_sel, down32), out_row, col_blocks)
    h_sel = jnp.take(hidden, out_row, axis=0).astype(jnp.float32)
    out_rows = place_terms(jnp.einsum("sri,sij->srj", h_sel, down32), out_col, row_blocks)
    prob_rows = jnp.sum(dy_t.astype(jnp.float32) * out_rows, axis=(0, 2)).astype(jnp.bfloat16)
    p32 = p_rows.astype(jnp.float32)[None, :, None]
    dh = p32 * m
    dg = (dh * u * sig * (1.0 + g * (1.0 - sig))).astype(jnp.bfloat16)
    du = (dh * act).astype(jnp.bfloat16)
    dg_sel = jnp.take(dg, in_col, axis=0).astype(jnp.float32)
    du_sel = jnp.take(du, in_col, axis=0).astype(jnp.float32)
    part = place_terms(jnp.einsum("srj,sij->sri", dg_sel, gate32), in_row, row_blocks)
    part = part + place_terms(jnp.einsum("srj,sij->sri", du_sel, up32), in_row, row_blocks)
    part = part.astype(jnp.bfloat16)
    scaled = (p32 * dy_t.astype(jnp.float32)).astype(jnp.bfloat16)
    q_sel = jnp.take(scaled, out_col, axis=0).astype(jnp.float32)
    in_live = live_in.astype(jnp.float32)[:, None, None]
    gate_part = jnp.einsum("sri,srj->sij", x_sel, dg_sel) * in_live
    up_part = jnp.einsum("sri,srj->sij", x_sel, du_sel) * in_live
    down_part = jnp.einsum("sri,srj->sij", h_sel, q_sel) * live_out.astype(jnp.float32)[:, None, None]
    return part, prob_rows, gate_part, up_part, down_part


def reference(tokens, cotangent, expert_ids, probs, gate_tiles, up_tiles, down_tiles, in_ids, in_count, out_ids, out_count):
    count = TOK_DEV * TOP
    row_blocks = D // TILE
    total = N_EXPERT * CAP
    dummy = DEVICES * count
    positions = jax.vmap(lambda block: slot_positions(block, CAP))(expert_ids.reshape(DEVICES, TOK_DEV, TOP))

    def make_table(pos):
        return jnp.full((EXPERTS * CAP,), count, jnp.int32).at[pos].set(jnp.arange(count, dtype=jnp.int32))

    tables = jax.vmap(make_table)(positions)
    offsets = (jnp.arange(DEVICES, dtype=jnp.int32) * count)[:, None]
    assign = jnp.where(tables < count, tables + offsets, dummy).astype(jnp.int32)
    assign = assign.reshape(N_EXPERT, N_FSDP, EXPERTS, CAP).transpose(2, 1, 0, 3).reshape(EXPERTS, N_FSDP, total)
    token_pad = jnp.concatenate([tokens, jnp.zeros((1, D), tokens.dtype)], axis=0).reshape(TOKENS + 1, row_blocks, TILE)
    cot_pad = jnp.concatenate([cotangent, jnp.zeros((1, D), cotangent.dtype)], axis=0).reshape(TOKENS + 1, row_blocks, TILE)
    prob_pad = jnp.concatenate([probs.reshape(-1), jnp.zeros((1,), probs.dtype)])

    def per_expert(carry, expert):
        grad_acc, prob_acc = carry
        live_in = live_slots(in_count[expert])
        live_out = live_slots(out_count[expert])
        in_mask = live_in.astype(jnp.bfloat16)[:, None, None]
        gate = gate_tiles[expert] * in_mask
        up = up_tiles[expert] * in_mask
        down = down_tiles[expert] * live_out.astype(jnp.bfloat16)[:, None, None]

        def per_group(grads, group):
            picked = assign[expert, group]
            token_index = jnp.where(picked < dummy, picked // TOP, TOKENS).astype(jnp.int32)
            x_t = jnp.take(token_pad, token_index, axis=0).transpose(1, 0, 2)
            dy_t = jnp.take(cot_pad, token_index, axis=0).transpose(1, 0, 2)
            p_rows = jnp.take(prob_pad, picked, axis=0)
            part, prob_rows, gate_part, up_part, down_part = expert_rows(x_t, dy_t, p_rows, gate, up, down, in_ids[expert], out_ids[expert], live_in, live_out)
            grads = (grads[0] + gate_part, grads[1] + up_part, grads[2] + down_part)
            return grads, (part, prob_rows, picked, token_index)

        empty = jnp.zeros((SLOTS, TILE, TILE), jnp.float32)
        grads, (parts, prob_rows, picked, token_index) = lax.scan(per_group, (empty, empty, empty), jnp.arange(N_FSDP, dtype=jnp.int32))
        rows_flat = parts.transpose(0, 2, 1, 3).reshape(N_FSDP * total, D).astype(jnp.float32)
        grad_acc = grad_acc.at[token_index.reshape(-1)].add(rows_flat)
        prob_acc = prob_acc.at[picked.reshape(-1)].set(prob_rows.reshape(-1))
        return (grad_acc, prob_acc), grads

    start = (jnp.zeros((TOKENS + 1, D), jnp.float32), jnp.zeros((dummy + 1,), jnp.bfloat16))
    (grad_acc, prob_acc), grads = lax.scan(per_expert, start, jnp.arange(EXPERTS, dtype=jnp.int32))
    token_grad = grad_acc[:TOKENS].astype(jnp.bfloat16)
    prob_grad = prob_acc[:dummy].reshape(TOKENS, TOP)
    return token_grad, prob_grad, grads[0], grads[1], grads[2]
```

```python
import functools

import jax
import jax.numpy as jnp
from jax import lax
from jax.experimental import pallas as pl
from jax.experimental.pallas import tpu as pltpu
from jax.sharding import Mesh
from jax.sharding import PartitionSpec as P

FF = 8192
TILE = 128
COL_BLOCKS = FF // TILE
EXPERTS = 8
NX = 4
NZ = 8
SLOTS = NX * NZ
CAP = 40
ROWS = 128
WIDTH = 3072
TOTAL = EXPERTS * CAP
PEERS = EXPERTS * NX
AHEAD = 16
IN_AT, OUT_AT, Z_AT, COUNT_AT, RANK_AT, PLAN = 0, 32, 64, 96, 128, 256

BF = jnp.bfloat16
F32 = jnp.float32
SMEM = pl.BlockSpec(memory_space=pltpu.SMEM)
VMEM = pl.BlockSpec(memory_space=pltpu.VMEM)
LIMIT = 48 * 1024 * 1024


def call(kernel, out, ins, outs, scratch=(), cost=None):
    return pl.pallas_call(
        kernel,
        out_shape=out,
        in_specs=ins,
        out_specs=outs,
        scratch_shapes=list(scratch),
        cost_estimate=cost,
        compiler_params=pltpu.CompilerParams(vmem_limit_bytes=LIMIT),
    )


def dot(a, b):
    return lax.dot_general(a, b, (((1,), (0,)), ((), ())), preferred_element_type=F32)


def dot_nt(a, b):
    return lax.dot_general(a, b, (((1,), (1,)), ((), ())), preferred_element_type=F32)


def dot_tn(a, b):
    return lax.dot_general(a, b, (((0,), (0,)), ((), ())), preferred_element_type=F32)


def back_tail(per):
    return 16 if per % 2 == 0 else 8


def plan_kernel(in_ids, in_count, out_ids, out_count, plan):
    def clear(i, _):
        plan[0, i] = 0
        return 0

    lax.fori_loop(0, PLAN, clear, 0)

    def step(i, rank):
        s = (i % NX) * NZ + i // NX
        live = jnp.logical_and(in_count[0, s] > 0, out_count[0, s] > 0)
        plan[0, RANK_AT + s] = jnp.where(live, rank, -1)

        @pl.when(live)
        def _():
            plan[0, IN_AT + rank] = in_ids[0, s] // COL_BLOCKS
            plan[0, OUT_AT + rank] = out_ids[0, s]
            plan[0, Z_AT + rank] = i // NX

        return rank + live.astype(jnp.int32)

    plan[0, COUNT_AT] = lax.fori_loop(0, SLOTS, step, jnp.int32(0))


def assignment(ids):
    experts = lax.broadcasted_iota(jnp.int32, (EXPERTS, ROWS), 0)
    first = ids[0:1, :] == experts
    second = ids[1:2, :] == experts
    named = jnp.logical_or(first, second)
    above = lax.broadcasted_iota(jnp.int32, (ROWS, ROWS), 0) < lax.broadcasted_iota(
        jnp.int32, (ROWS, ROWS), 1
    )
    place = dot(named.astype(F32).astype(BF), above.astype(F32).astype(BF))
    return first, second, jnp.where(named, place, -1.0)


def one_hot(place):
    at = lax.broadcasted_iota(jnp.int32, (CAP, ROWS), 0).astype(F32)
    rows = [(place[e : e + 1, :] == at).astype(F32) for e in range(EXPERTS)]
    return jnp.concatenate(rows, axis=0).astype(BF)


def dispatch_kernel(per, plans, ids, probs, tokens, cot, out, xs, ys, prob_rows, places):
    first, second, place = assignment(ids[...])
    p = probs[...].astype(F32)
    prob_rows[...] = jnp.where(first, p[0:1, :], 0.0) + jnp.where(second, p[1:2, :], 0.0)
    places[...] = place
    pick = one_hot(place)
    for j in range(WIDTH // 256):
        at = slice(j * 256, (j + 1) * 256)
        xs[:, at] = dot(pick, tokens[:, at])
        ys[:, at] = dot(pick, cot[:, at])
    line = lax.broadcasted_iota(jnp.int32, (AHEAD, ROWS), 0)

    def per_expert(e, _):
        rows = pl.ds(pl.multiple_of(e * CAP, 8), CAP)
        extra = jnp.where(
            line == 0,
            prob_rows[pl.ds(e, 1), :],
            jnp.where(line == 1, places[pl.ds(e, 1), :], 0.0),
        ).astype(BF)
        for x in range(NX):
            for k in range(per):
                r = k * NX + x
                at_in = pl.multiple_of(plans[e, IN_AT + r] * TILE, TILE)
                at_out = pl.multiple_of(plans[e, OUT_AT + r] * TILE, TILE)
                both = jnp.concatenate(
                    [xs[rows, pl.ds(at_in, TILE)], ys[rows, pl.ds(at_out, TILE)]], axis=0
                )
                out[e * NX + x, 2 * CAP * k : 2 * CAP * (k + 1), :] = both.astype(BF)
            out[e * NX + x, 2 * CAP * per : 2 * CAP * per + AHEAD, :] = extra
        return 0

    lax.fori_loop(0, EXPERTS, per_expert, 0)


def pick_weights_kernel(plan, place, own, one, two, three, out):
    x, z = place[0], place[1]
    out[...] = jnp.zeros_like(out)
    for shift, source in enumerate((own, one, two, three)):
        home = lax.rem(x + NX - shift, NX)
        rank = plan[0, RANK_AT + home * NZ + z]

        @pl.when(jnp.logical_and(rank >= 0, lax.rem(rank + NX, NX) == x))
        def _():
            out[...] = source[...]


def pick_grads_kernel(plan, place, own, one, two, three, gate, up, down):
    x, z = place[0], place[1]
    rank = plan[0, RANK_AT + x * NZ + z]
    outs = (gate, up, down)
    for ref in outs:
        ref[...] = jnp.zeros_like(ref)
    for shift, source in enumerate((own, one, two, three)):
        home = lax.rem(x + NX - shift, NX)

        @pl.when(jnp.logical_and(rank >= 0, lax.rem(rank + NX, NX) == home))
        def _():
            for i, ref in enumerate(outs):
                ref[0, 0] = source[i]


def expert_kernel(per, plan, place, got, weights, back, grads, pair, down, pair_sum, down_sum):
    x = place[0]
    count = plan[0, COUNT_AT]
    for k in range(per):
        z = plan[0, Z_AT + k * NX + x]
        live = jnp.where(k * NX + x < count, 1.0, 0.0).astype(F32)
        for i in range(2):
            tile = weights[3 * z + i].astype(F32) * live
            pair[k, :, i * TILE : (i + 1) * TILE] = tile.astype(BF)
        down[k] = (weights[3 * z + 2].astype(F32) * live).astype(BF)
    pair_sum[...] = jnp.zeros_like(pair_sum)
    down_sum[...] = jnp.zeros_like(down_sum)
    group = 8
    rows = group * CAP
    tail = back_tail(per)
    ones = jnp.ones((ROWS, TILE), BF)

    def chunk(c, _):
        at = pl.ds(c * group, group)
        extra = got[at, 2 * CAP * per : 2 * CAP * per + AHEAD, :].astype(F32)
        slot = lax.broadcasted_iota(jnp.int32, (group, CAP, ROWS), 1).astype(F32)
        mine = extra[:, 1:2, :] == slot
        p = dot(jnp.where(mine, extra[:, 0:1, :], 0.0).reshape(rows, ROWS).astype(BF), ones)
        inner = jnp.zeros((rows, TILE), F32)
        pieces = []
        for k in range(per):
            both = got[at, 2 * CAP * k : 2 * CAP * (k + 1), :].astype(F32)
            rows_x = both[:, :CAP, :].reshape(rows, TILE).astype(BF)
            rows_dy = both[:, CAP:, :].reshape(rows, TILE)
            gu = dot(rows_x, pair[k])
            g, u = gu[:, :TILE], gu[:, TILE:]
            m = dot_nt(rows_dy.astype(BF), down[k])
            sig = jax.nn.sigmoid(g)
            act = g * sig
            h = (act * u).astype(BF)
            inner = inner + h.astype(F32) * m
            dh = p * m
            dg = (dh * u * sig * (1.0 + g * (1.0 - sig))).astype(BF)
            du = (dh * act).astype(BF)
            q = (p * rows_dy).astype(BF)
            dgu = jnp.concatenate([dg, du], axis=1)
            pieces.append(dot_nt(dgu, pair[k]).reshape(group, CAP, TILE))
            pair_sum[k] += dot_tn(rows_x, dgu)
            down_sum[k] += dot_tn(h, q)
        column = jnp.sum(inner, axis=1, keepdims=True).reshape(group, CAP, 1)
        row = jnp.sum(jnp.where(mine, column, 0.0), axis=1, keepdims=True)
        high = row.astype(BF).astype(F32)
        line = lax.broadcasted_iota(jnp.int32, (group, tail, ROWS), 1)
        pieces.append(jnp.where(line == 0, high, jnp.where(line == 1, row - high, 0.0)))
        back[at] = jnp.concatenate(pieces, axis=1).astype(BF)
        return 0

    lax.fori_loop(0, PEERS // group, chunk, 0)
    grads[...] = jnp.zeros_like(grads)
    for k in range(per):
        z = plan[0, Z_AT + k * NX + x]

        @pl.when(k * NX + x < count)
        def _():
            grads[3 * z] = pair_sum[k, :, :TILE]
            grads[3 * z + 1] = pair_sum[k, :, TILE:]
            grads[3 * z + 2] = down_sum[k]


def combine_kernel(per, plans, ids, back, token_grad, prob_grad, parts, prob_rows):
    tail = back_tail(per)
    parts[...] = jnp.zeros_like(parts)

    def per_expert(e, _):
        rows = pl.ds(pl.multiple_of(e * CAP, 8), CAP)
        total = jnp.zeros((1, ROWS), F32)
        for x in range(NX):
            chunk = back[e * NX + x].astype(F32)
            for k in range(per):
                at = pl.multiple_of(plans[e, IN_AT + k * NX + x] * TILE, TILE)
                parts[rows, pl.ds(at, TILE)] += chunk[CAP * k : CAP * (k + 1), :]
            total = total + chunk[CAP * per : CAP * per + 1] + chunk[CAP * per + 1 : CAP * per + 2]
        prob_rows[pl.ds(e, 1), :] = total
        return 0

    lax.fori_loop(0, EXPERTS, per_expert, 0)
    first, second, place = assignment(ids[...])
    pick = one_hot(place)
    for j in range(WIDTH // 256):
        at = slice(j * 256, (j + 1) * 256)
        token_grad[:, at] = dot_tn(pick, parts[:, at].astype(BF)).astype(BF)
    rows = prob_rows[...]
    prob_grad[0:1, :] = jnp.sum(jnp.where(first, rows, 0.0), axis=0, keepdims=True)
    prob_grad[1:2, :] = jnp.sum(jnp.where(second, rows, 0.0), axis=0, keepdims=True)


def exchange(values, axes):
    return lax.all_to_all(values, axes, split_axis=0, concat_axis=0, tiled=True)


def shifted(values):
    return [
        lax.ppermute(values, "x", [(i, (i + shift) % NX) for i in range(NX)])
        for shift in range(1, NX)
    ]


def rest(per, plan, plans, place, ids, probs, tokens, cotangent, weights):
    shape = jax.ShapeDtypeStruct
    ahead = 2 * CAP * per + AHEAD
    behind = CAP * per + back_tail(per)
    sent = call(
        functools.partial(dispatch_kernel, per),
        shape((PEERS, ahead, TILE), BF),
        [SMEM, VMEM, VMEM, VMEM, VMEM],
        VMEM,
        [
            pltpu.VMEM((TOTAL, WIDTH), F32),
            pltpu.VMEM((TOTAL, WIDTH), F32),
            pltpu.VMEM((EXPERTS, ROWS), F32),
            pltpu.VMEM((EXPERTS, ROWS), F32),
        ],
    )(plans, ids, probs, tokens, cotangent)
    got = exchange(sent, ("expert", "x"))
    weights = lax.all_gather(weights, "z", axis=0, tiled=True)
    back, grads = call(
        functools.partial(expert_kernel, per),
        (shape((PEERS, behind, TILE), BF), shape((3 * NZ, TILE, TILE), F32)),
        [SMEM, SMEM, VMEM, VMEM],
        (VMEM, VMEM),
        [
            pltpu.VMEM((per, TILE, 2 * TILE), BF),
            pltpu.VMEM((per, TILE, TILE), BF),
            pltpu.VMEM((per, TILE, 2 * TILE), F32),
            pltpu.VMEM((per, TILE, TILE), F32),
        ],
    )(plan, place, got, weights)
    grads = lax.psum_scatter(grads, "z", scatter_dimension=0, tiled=True)
    returned = exchange(back, ("expert", "x"))
    token_grad, prob_grad = call(
        functools.partial(combine_kernel, per),
        (shape((ROWS, WIDTH), BF), shape((2, ROWS), F32)),
        [SMEM, VMEM, VMEM],
        (VMEM, VMEM),
        [pltpu.VMEM((TOTAL, WIDTH), F32), pltpu.VMEM((EXPERTS, ROWS), F32)],
    )(plans, ids, returned)
    tile = shape((1, 1, TILE, TILE), F32)
    gate, up, down = call(
        pick_grads_kernel,
        (tile, tile, tile),
        [SMEM, SMEM, VMEM, VMEM, VMEM, VMEM],
        (VMEM, VMEM, VMEM),
    )(plan, place, grads, *shifted(grads))
    return token_grad, prob_grad, gate, up, down


def local(
    tokens,
    cotangent,
    expert_ids,
    probs,
    gate_tiles,
    up_tiles,
    down_tiles,
    in_ids,
    in_count,
    out_ids,
    out_count,
):
    shape = jax.ShapeDtypeStruct
    plan = call(plan_kernel, shape((1, PLAN), jnp.int32), [SMEM] * 4, SMEM)(
        in_ids, in_count, out_ids, out_count
    )
    plans = exchange(jnp.broadcast_to(plan, (EXPERTS, PLAN)), "expert")
    place = jnp.stack([lax.axis_index("x"), lax.axis_index("z")]).astype(jnp.int32)
    ids = expert_ids.T
    rows = probs.T
    own = jnp.concatenate([gate_tiles[0], up_tiles[0], down_tiles[0]], axis=0)
    weights = call(
        pick_weights_kernel,
        shape((3, TILE, TILE), BF),
        [SMEM, SMEM, VMEM, VMEM, VMEM, VMEM],
        VMEM,
    )(plan, place, own, *shifted(own))
    most = jnp.max(plans[:, COUNT_AT])
    sizes = (3, 4, 8)
    which = sum((most > NX * size).astype(jnp.int32) for size in sizes[:-1])
    token_grad, prob_grad, gate, up, down = lax.switch(
        which,
        [functools.partial(rest, size) for size in sizes],
        plan,
        plans,
        place,
        ids,
        rows,
        tokens,
        cotangent,
        weights,
    )
    return token_grad, prob_grad.T.astype(BF), gate, up, down


def solution(mesh):
    finer = Mesh(mesh.devices.reshape(EXPERTS, NX, NZ), ("expert", "x", "z"))
    rows = P(("expert", "x", "z"), None)
    tiles = P("expert", ("x", "z"), None, None)
    table = P("expert", None)
    return jax.shard_map(
        local,
        mesh=finer,
        in_specs=(rows, rows, rows, rows, tiles, tiles, tiles, table, table, table, table),
        out_specs=(rows, rows, tiles, tiles, tiles),
        check_vma=False,
    )
```

```python
import functools

import jax
import jax.numpy as jnp
from jax import lax
from jax.experimental import pallas as pl
from jax.experimental.pallas import tpu as pltpu
from jax.sharding import Mesh
from jax.sharding import PartitionSpec as P

FF = 8192
TILE = 128
COL_BLOCKS = FF // TILE
EXPERTS = 8
NX = 4
NZ = 8
SLOTS = NX * NZ
CAP = 40
ROWS = 128
WIDTH = 3072
TOTAL = EXPERTS * CAP
PEERS = EXPERTS * NX
AHEAD = 16
IN_AT, OUT_AT, Z_AT, COUNT_AT, RANK_AT, BRANCH_AT = range(6)
SIZES = (3, 4, 8)

BF = jnp.bfloat16
F32 = jnp.float32
SMEM = pl.BlockSpec(memory_space=pltpu.SMEM)
VMEM = pl.BlockSpec(memory_space=pltpu.VMEM)
LIMIT = 48 * 1024 * 1024


def call(kernel, out, ins, outs, scratch=(), cost=None):
    return pl.pallas_call(
        kernel,
        out_shape=out,
        in_specs=ins,
        out_specs=outs,
        scratch_shapes=list(scratch),
        cost_estimate=cost,
        compiler_params=pltpu.CompilerParams(vmem_limit_bytes=LIMIT),
    )


def dot(a, b):
    return lax.dot_general(a, b, (((1,), (0,)), ((), ())), preferred_element_type=F32)


def dot_nt(a, b):
    return lax.dot_general(a, b, (((1,), (1,)), ((), ())), preferred_element_type=F32)


def dot_tn(a, b):
    return lax.dot_general(a, b, (((0,), (0,)), ((), ())), preferred_element_type=F32)


def back_tail(per):
    return 16 if per % 2 == 0 else 8


def plan_kernel(counts, plan, copies):
    slot_i = lax.broadcasted_iota(jnp.int32, (SLOTS, SLOTS), 0)
    slot_j = lax.broadcasted_iota(jnp.int32, (SLOTS, SLOTS), 1)
    order_i = (slot_i & (NZ - 1)) * NX + (slot_i >> 3)
    order_j = (slot_j & (NZ - 1)) * NX + (slot_j >> 3)

    def column(line):
        return jnp.sum(jnp.where(slot_i == slot_j, line, 0.0), axis=1, keepdims=True)

    live = jnp.logical_and(counts[1:2, :] > 0, counts[3:4, :] > 0).astype(F32)
    rank = jnp.sum(jnp.where(order_j < order_i, live, 0.0), axis=1, keepdims=True)
    live_column = column(live)
    hot = jnp.logical_and(rank == slot_j.astype(F32), live_column > 0.0)

    def by_rank(values):
        return jnp.sum(jnp.where(hot, values, 0.0), axis=0, keepdims=True)

    rank_line = jnp.sum(jnp.where(order_i < order_j, live_column, 0.0), axis=0, keepdims=True)
    count = jnp.sum(live, axis=1, keepdims=True) + jnp.zeros_like(live)
    branch = jnp.zeros_like(live)
    for size in SIZES[:-1]:
        branch = branch + (count > NX * size).astype(F32)
    plan[...] = jnp.zeros_like(plan)
    for at, line in (
        (IN_AT, by_rank(column((counts[0:1, :] >> 6).astype(F32)))),
        (OUT_AT, by_rank(column(counts[2:3, :].astype(F32)))),
        (Z_AT, by_rank((slot_i & (NZ - 1)).astype(F32))),
        (COUNT_AT, count),
        (RANK_AT, jnp.where(live > 0.0, rank_line, -1.0)),
        (BRANCH_AT, branch),
    ):
        plan[at : at + 1, :SLOTS] = line.astype(jnp.int32)
    whole = plan[...]
    for e in range(EXPERTS):
        copies[e] = whole


def assignment(ids):
    experts = lax.broadcasted_iota(jnp.int32, (EXPERTS, ROWS), 0)
    first = ids[0:1, :] == experts
    second = ids[1:2, :] == experts
    named = jnp.logical_or(first, second)
    above = lax.broadcasted_iota(jnp.int32, (ROWS, ROWS), 0) < lax.broadcasted_iota(
        jnp.int32, (ROWS, ROWS), 1
    )
    place = dot(named.astype(F32).astype(BF), above.astype(F32).astype(BF))
    return first, second, jnp.where(named, place, -1.0)


def one_hot(place):
    at = lax.broadcasted_iota(jnp.int32, (CAP, ROWS), 0).astype(F32)
    rows = [(place[e : e + 1, :] == at).astype(F32) for e in range(EXPERTS)]
    return jnp.concatenate(rows, axis=0).astype(BF)


def dispatch_kernel(per, plans, ids, probs, tokens, cot, out, xs, ys, prob_rows, places):
    first, second, place = assignment(ids[...])
    p = probs[...].astype(F32)
    prob_rows[...] = jnp.where(first, p[0:1, :], 0.0) + jnp.where(second, p[1:2, :], 0.0)
    places[...] = place
    pick = one_hot(place)
    for j in range(WIDTH // 256):
        at = slice(j * 256, (j + 1) * 256)
        xs[:, at] = dot(pick, tokens[:, at])
        ys[:, at] = dot(pick, cot[:, at])
    line = lax.broadcasted_iota(jnp.int32, (AHEAD, ROWS), 0)

    def per_expert(e, _):
        rows = pl.ds(pl.multiple_of(e * CAP, 8), CAP)
        extra = jnp.where(
            line == 0,
            prob_rows[pl.ds(e, 1), :],
            jnp.where(line == 1, places[pl.ds(e, 1), :], 0.0),
        ).astype(BF)
        for x in range(NX):
            for k in range(per):
                r = k * NX + x
                at_in = pl.multiple_of(plans[e, IN_AT, r] * TILE, TILE)
                at_out = pl.multiple_of(plans[e, OUT_AT, r] * TILE, TILE)
                both = jnp.concatenate(
                    [xs[rows, pl.ds(at_in, TILE)], ys[rows, pl.ds(at_out, TILE)]], axis=0
                )
                out[e * NX + x, 2 * CAP * k : 2 * CAP * (k + 1), :] = both.astype(BF)
            out[e * NX + x, 2 * CAP * per : 2 * CAP * per + AHEAD, :] = extra
        return 0

    lax.fori_loop(0, EXPERTS, per_expert, 0)


def pick_weights_kernel(plan, place, own, one, two, three, out):
    x, z = place[0], place[1]
    out[...] = jnp.zeros_like(out)
    for shift, source in enumerate((own, one, two, three)):
        home = lax.rem(x + NX - shift, NX)
        rank = plan[RANK_AT, home * NZ + z]

        @pl.when(jnp.logical_and(rank >= 0, lax.rem(rank + NX, NX) == x))
        def _():
            out[...] = source[...]


def pick_grads_kernel(plan, place, own, one, two, three, gate, up, down):
    x, z = place[0], place[1]
    rank = plan[RANK_AT, x * NZ + z]
    outs = (gate, up, down)
    for ref in outs:
        ref[...] = jnp.zeros_like(ref)
    for shift, source in enumerate((own, one, two, three)):
        home = lax.rem(x + NX - shift, NX)

        @pl.when(jnp.logical_and(rank >= 0, lax.rem(rank + NX, NX) == home))
        def _():
            for i, ref in enumerate(outs):
                ref[0, 0] = source[i].astype(F32)


def expert_kernel(per, plan, place, got, weights, back, *refs):
    grads, (pair, down, pair_sum, down_sum) = refs[:NZ], refs[NZ:]
    x, own_z = place[0], place[1]
    count = plan[COUNT_AT, 0]
    for k in range(per):
        z = plan[Z_AT, k * NX + x]
        live = jnp.where(k * NX + x < count, 1.0, 0.0).astype(F32)
        for i in range(2):
            tile = weights[3 * z + i].astype(F32) * live
            pair[k, :, i * TILE : (i + 1) * TILE] = tile.astype(BF)
        down[k] = (weights[3 * z + 2].astype(F32) * live).astype(BF)
    pair_sum[...] = jnp.zeros_like(pair_sum)
    down_sum[...] = jnp.zeros_like(down_sum)
    group = 8
    rows = group * CAP
    tail = back_tail(per)
    ones = jnp.ones((ROWS, TILE), BF)

    def chunk(c, _):
        at = pl.ds(c * group, group)
        extra = got[at, 2 * CAP * per : 2 * CAP * per + AHEAD, :].astype(F32)
        slot = lax.broadcasted_iota(jnp.int32, (group, CAP, ROWS), 1).astype(F32)
        mine = extra[:, 1:2, :] == slot
        p = dot(jnp.where(mine, extra[:, 0:1, :], 0.0).reshape(rows, ROWS).astype(BF), ones)
        inner = jnp.zeros((rows, TILE), F32)
        pieces = []
        for k in range(per):
            both = got[at, 2 * CAP * k : 2 * CAP * (k + 1), :].astype(F32)
            rows_x = both[:, :CAP, :].reshape(rows, TILE).astype(BF)
            rows_dy = both[:, CAP:, :].reshape(rows, TILE)
            gu = dot(rows_x, pair[k])
            g, u = gu[:, :TILE], gu[:, TILE:]
            m = dot_nt(rows_dy.astype(BF), down[k])
            sig = jax.nn.sigmoid(g)
            act = g * sig
            h = (act * u).astype(BF)
            inner = inner + h.astype(F32) * m
            dh = p * m
            dg = (dh * u * sig * (1.0 + g * (1.0 - sig))).astype(BF)
            du = (dh * act).astype(BF)
            q = (p * rows_dy).astype(BF)
            dgu = jnp.concatenate([dg, du], axis=1)
            pieces.append(dot_nt(dgu, pair[k]).reshape(group, CAP, TILE))
            pair_sum[k] += dot_tn(rows_x, dgu)
            down_sum[k] += dot_tn(h, q)
        column = jnp.sum(inner, axis=1, keepdims=True).reshape(group, CAP, 1)
        row = jnp.sum(jnp.where(mine, column, 0.0), axis=1, keepdims=True)
        high = row.astype(BF).astype(F32)
        line = lax.broadcasted_iota(jnp.int32, (group, tail, ROWS), 1)
        pieces.append(jnp.where(line == 0, high, jnp.where(line == 1, row - high, 0.0)))
        back[at] = jnp.concatenate(pieces, axis=1).astype(BF)
        return 0

    lax.fori_loop(0, PEERS // group, chunk, 0)
    for ref in grads:
        ref[...] = jnp.zeros_like(ref)
    for k in range(per):
        z = plan[Z_AT, k * NX + x]
        for shift, ref in enumerate(grads):

            @pl.when(jnp.logical_and(k * NX + x < count, (z - own_z) & (NZ - 1) == shift))
            def _():
                ref[0] = pair_sum[k, :, :TILE].astype(ref.dtype)
                ref[1] = pair_sum[k, :, TILE:].astype(ref.dtype)
                ref[2] = down_sum[k].astype(ref.dtype)


def sum_kernel(own, *refs):
    total = own[...]
    for ref in refs[:-2]:
        total = total + ref[...].astype(F32)
    refs[-2][...] = total
    refs[-1][...] = total.astype(BF)


def combine_kernel(per, plans, ids, back, token_grad, prob_grad, parts, prob_rows):
    tail = back_tail(per)
    parts[...] = jnp.zeros_like(parts)

    def per_expert(e, _):
        rows = pl.ds(pl.multiple_of(e * CAP, 8), CAP)
        total = jnp.zeros((1, ROWS), F32)
        for x in range(NX):
            chunk = back[e * NX + x].astype(F32)
            for k in range(per):
                at = pl.multiple_of(plans[e, IN_AT, k * NX + x] * TILE, TILE)
                parts[rows, pl.ds(at, TILE)] += chunk[CAP * k : CAP * (k + 1), :]
            total = total + chunk[CAP * per : CAP * per + 1] + chunk[CAP * per + 1 : CAP * per + 2]
        prob_rows[pl.ds(e, 1), :] = total
        return 0

    lax.fori_loop(0, EXPERTS, per_expert, 0)
    first, second, place = assignment(ids[...])
    pick = one_hot(place)
    for j in range(WIDTH // 256):
        at = slice(j * 256, (j + 1) * 256)
        token_grad[:, at] = dot_tn(pick, parts[:, at].astype(BF)).astype(BF)
    rows = prob_rows[...]
    prob_grad[...] = jnp.concatenate(
        [
            jnp.sum(jnp.where(first, rows, 0.0), axis=0, keepdims=True),
            jnp.sum(jnp.where(second, rows, 0.0), axis=0, keepdims=True),
        ],
        axis=0,
    ).astype(BF)


def exchange(values, axes):
    return lax.all_to_all(values, axes, split_axis=0, concat_axis=0, tiled=True)


def moved(values, axis, shift):
    size = lax.axis_size(axis)
    return lax.ppermute(values, axis, [(i, (i + shift) % size) for i in range(size)])


def rest(per, plan, plans, place, ids, probs, tokens, cotangent, weights):
    shape = jax.ShapeDtypeStruct
    triple = (3, TILE, TILE)
    ahead = 2 * CAP * per + AHEAD
    behind = CAP * per + back_tail(per)
    sent = call(
        functools.partial(dispatch_kernel, per),
        shape((PEERS, ahead, TILE), BF),
        [SMEM, VMEM, VMEM, VMEM, VMEM],
        VMEM,
        [
            pltpu.VMEM((TOTAL, WIDTH), F32),
            pltpu.VMEM((TOTAL, WIDTH), F32),
            pltpu.VMEM((EXPERTS, ROWS), F32),
            pltpu.VMEM((EXPERTS, ROWS), F32),
        ],
    )(plans, ids, probs, tokens, cotangent)
    got = exchange(sent, ("expert", "x"))
    weights = lax.all_gather(weights, "z", axis=0, tiled=True)
    back, *grads = call(
        functools.partial(expert_kernel, per),
        (shape((PEERS, behind, TILE), BF), shape(triple, F32), *[shape(triple, BF)] * (NZ - 1)),
        [SMEM, SMEM, VMEM, VMEM],
        [VMEM] * (NZ + 1),
        [
            pltpu.VMEM((per, TILE, 2 * TILE), BF),
            pltpu.VMEM((per, TILE, TILE), BF),
            pltpu.VMEM((per, TILE, 2 * TILE), F32),
            pltpu.VMEM((per, TILE, TILE), F32),
        ],
    )(plan, place, got, weights)
    returned = exchange(back, ("expert", "x"))
    terms = [grads[0]] + [moved(grads[shift], "z", shift) for shift in (1, 7, 2, 6, 3, 5, 4)]
    own, sent = call(sum_kernel, (shape(triple, F32), shape(triple, BF)), [VMEM] * NZ, (VMEM, VMEM))(
        *terms
    )
    token_grad, prob_grad = call(
        functools.partial(combine_kernel, per),
        (shape((ROWS, WIDTH), BF), shape((2, ROWS), BF)),
        [SMEM, VMEM, VMEM],
        (VMEM, VMEM),
        [pltpu.VMEM((TOTAL, WIDTH), F32), pltpu.VMEM((EXPERTS, ROWS), F32)],
    )(plans, ids, returned)
    tile = shape((1, 1, TILE, TILE), F32)
    gate, up, down = call(
        pick_grads_kernel,
        (tile, tile, tile),
        [SMEM, SMEM, VMEM, VMEM, VMEM, VMEM],
        (VMEM, VMEM, VMEM),
    )(plan, place, own, *[moved(sent, "x", shift) for shift in range(1, NX)])
    return token_grad, prob_grad, gate, up, down


def local(
    tokens,
    cotangent,
    expert_ids,
    probs,
    gate_tiles,
    up_tiles,
    down_tiles,
    in_ids,
    in_count,
    out_ids,
    out_count,
):
    shape = jax.ShapeDtypeStruct
    counts = jnp.concatenate([in_ids, in_count, out_ids, out_count], axis=0)
    plan, copies = call(
        plan_kernel,
        (shape((8, 128), jnp.int32), shape((EXPERTS, 8, 128), jnp.int32)),
        [VMEM],
        (VMEM, VMEM),
    )(counts)
    plans = exchange(copies, "expert")
    which = jnp.max(plans[:, BRANCH_AT, 0])
    place = jnp.stack([lax.axis_index("x"), lax.axis_index("z")]).astype(jnp.int32)
    ids = expert_ids.T
    rows = probs.T
    plan, *three = lax.optimization_barrier((plan, gate_tiles, up_tiles, down_tiles))
    own = jnp.concatenate([tile[0] for tile in three], axis=0)
    weights = call(
        pick_weights_kernel,
        shape((3, TILE, TILE), BF),
        [SMEM, SMEM, VMEM, VMEM, VMEM, VMEM],
        VMEM,
    )(plan, place, own, *[moved(own, "x", shift) for shift in range(1, NX)])
    token_grad, prob_grad, gate, up, down = lax.switch(
        which,
        [functools.partial(rest, size) for size in SIZES],
        plan,
        plans,
        place,
        ids,
        rows,
        tokens,
        cotangent,
        weights,
    )
    return token_grad, prob_grad.T, gate, up, down


def solution(mesh):
    finer = Mesh(mesh.devices.reshape(EXPERTS, NX, NZ), ("expert", "x", "z"))
    rows = P(("expert", "x", "z"), None)
    tiles = P("expert", ("x", "z"), None, None)
    table = P("expert", None)
    return jax.shard_map(
        local,
        mesh=finer,
        in_specs=(rows, rows, rows, rows, tiles, tiles, tiles, table, table, table, table),
        out_specs=(rows, rows, tiles, tiles, tiles),
        check_vma=False,
    )
```

```python
import functools

import jax
import jax.numpy as jnp
from jax import lax
from jax.experimental import pallas as pl
from jax.experimental.pallas import tpu as pltpu
from jax.sharding import Mesh
from jax.sharding import PartitionSpec as P

FF = 8192
TILE = 128
COL_BLOCKS = FF // TILE
EXPERTS = 8
NX = 4
NZ = 8
SLOTS = NX * NZ
CAP = 40
ROWS = 128
WIDTH = 3072
TOTAL = EXPERTS * CAP
PEERS = EXPERTS * NX
AHEAD = 16
IN_AT, OUT_AT, Z_AT, COUNT_AT, RANK_AT, BRANCH_AT = range(6)
SIZES = (3, 4, 8)

BF = jnp.bfloat16
F32 = jnp.float32
SMEM = pl.BlockSpec(memory_space=pltpu.SMEM)
VMEM = pl.BlockSpec(memory_space=pltpu.VMEM)
HBM = pl.BlockSpec(memory_space=pltpu.HBM)
LIMIT = 40 * 1024 * 1024


def call(kernel, out, ins, outs, scratch=(), cost=None):
    return pl.pallas_call(
        kernel,
        out_shape=out,
        in_specs=ins,
        out_specs=outs,
        scratch_shapes=list(scratch),
        cost_estimate=cost,
        compiler_params=pltpu.CompilerParams(vmem_limit_bytes=LIMIT),
    )


def dot(a, b):
    return lax.dot_general(a, b, (((1,), (0,)), ((), ())), preferred_element_type=F32)


def dot_nt(a, b):
    return lax.dot_general(a, b, (((1,), (1,)), ((), ())), preferred_element_type=F32)


def dot_tn(a, b):
    return lax.dot_general(a, b, (((0,), (0,)), ((), ())), preferred_element_type=F32)


def back_tail(per):
    return 16 if per % 2 == 0 else 8


def plan_kernel(counts, plan, copies):
    slot_i = lax.broadcasted_iota(jnp.int32, (SLOTS, SLOTS), 0)
    slot_j = lax.broadcasted_iota(jnp.int32, (SLOTS, SLOTS), 1)
    order_i = (slot_i & (NZ - 1)) * NX + (slot_i >> 3)
    order_j = (slot_j & (NZ - 1)) * NX + (slot_j >> 3)

    def column(line):
        return jnp.sum(jnp.where(slot_i == slot_j, line, 0.0), axis=1, keepdims=True)

    live = jnp.logical_and(counts[1:2, :] > 0, counts[3:4, :] > 0).astype(F32)
    rank = jnp.sum(jnp.where(order_j < order_i, live, 0.0), axis=1, keepdims=True)
    live_column = column(live)
    hot = jnp.logical_and(rank == slot_j.astype(F32), live_column > 0.0)

    def by_rank(values):
        return jnp.sum(jnp.where(hot, values, 0.0), axis=0, keepdims=True)

    rank_line = jnp.sum(jnp.where(order_i < order_j, live_column, 0.0), axis=0, keepdims=True)
    count = jnp.sum(live, axis=1, keepdims=True) + jnp.zeros_like(live)
    branch = jnp.zeros_like(live)
    for size in SIZES[:-1]:
        branch = branch + (count > NX * size).astype(F32)
    plan[...] = jnp.zeros_like(plan)
    for at, line in (
        (IN_AT, by_rank(column((counts[0:1, :] >> 6).astype(F32)))),
        (OUT_AT, by_rank(column(counts[2:3, :].astype(F32)))),
        (Z_AT, by_rank((slot_i & (NZ - 1)).astype(F32))),
        (COUNT_AT, count),
        (RANK_AT, jnp.where(live > 0.0, rank_line, -1.0)),
        (BRANCH_AT, branch),
    ):
        plan[at : at + 1, :SLOTS] = line.astype(jnp.int32)
    whole = plan[...]
    for e in range(EXPERTS):
        copies[e] = whole


def assignment(ids):
    experts = lax.broadcasted_iota(jnp.int32, (EXPERTS, ROWS), 0)
    first = ids[0:1, :] == experts
    second = ids[1:2, :] == experts
    named = jnp.logical_or(first, second)
    above = lax.broadcasted_iota(jnp.int32, (ROWS, ROWS), 0) < lax.broadcasted_iota(
        jnp.int32, (ROWS, ROWS), 1
    )
    place = dot(named.astype(F32).astype(BF), above.astype(F32).astype(BF))
    return first, second, jnp.where(named, place, -1.0)


def one_hot(place):
    at = lax.broadcasted_iota(jnp.int32, (CAP, ROWS), 0).astype(F32)
    rows = [(place[e : e + 1, :] == at).astype(F32) for e in range(EXPERTS)]
    return jnp.concatenate(rows, axis=0).astype(BF)


def dispatch_kernel(per, plans, ids, probs, tokens, cot, sent, xs, ys, prob_rows, places, out, sem):
    first, second, place = assignment(ids[...])
    p = probs[...].astype(F32)
    prob_rows[...] = jnp.where(first, p[0:1, :], 0.0) + jnp.where(second, p[1:2, :], 0.0)
    places[...] = place
    pick = one_hot(place)
    for j in range(WIDTH // 256):
        at = slice(j * 256, (j + 1) * 256)
        xs[:, at] = dot(pick, tokens[:, at])
        ys[:, at] = dot(pick, cot[:, at])
    line = lax.broadcasted_iota(jnp.int32, (AHEAD, ROWS), 0)

    def per_expert(e, _):
        rows = pl.ds(pl.multiple_of(e * CAP, 8), CAP)
        extra = jnp.where(
            line == 0,
            prob_rows[pl.ds(e, 1), :],
            jnp.where(line == 1, places[pl.ds(e, 1), :], 0.0),
        ).astype(BF)
        for x in range(NX):
            for k in range(per):
                r = k * NX + x
                at_in = pl.multiple_of(plans[e, IN_AT, r] * TILE, TILE)
                at_out = pl.multiple_of(plans[e, OUT_AT, r] * TILE, TILE)
                both = jnp.concatenate(
                    [xs[rows, pl.ds(at_in, TILE)], ys[rows, pl.ds(at_out, TILE)]], axis=0
                )
                out[e * NX + x, 2 * CAP * k : 2 * CAP * (k + 1), :] = both.astype(BF)
            out[e * NX + x, 2 * CAP * per : 2 * CAP * per + AHEAD, :] = extra
        leave(e).start()
        return 0

    def leave(e):
        part = pl.ds(e * NX, NX)
        return pltpu.make_async_copy(out.at[part], sent.at[part], sem.at[e])

    def wait(e, _):
        leave(e).wait()
        return 0

    lax.fori_loop(0, EXPERTS, per_expert, 0)
    lax.fori_loop(0, EXPERTS, wait, 0)


def pick_weights_kernel(plan, place, own, one, two, three, out):
    x, z = place[0], place[1]
    out[...] = jnp.zeros_like(out)
    for shift, source in enumerate((own, one, two, three)):
        home = lax.rem(x + NX - shift, NX)
        rank = plan[RANK_AT, home * NZ + z]

        @pl.when(jnp.logical_and(rank >= 0, lax.rem(rank + NX, NX) == x))
        def _():
            out[...] = source[...]


def pick_grads_kernel(plan, place, own, one, two, three, gate, up, down):
    x, z = place[0], place[1]
    rank = plan[RANK_AT, x * NZ + z]
    outs = (gate, up, down)
    for ref in outs:
        ref[...] = jnp.zeros_like(ref)
    for shift, source in enumerate((own, one, two, three)):
        home = lax.rem(x + NX - shift, NX)

        @pl.when(jnp.logical_and(rank >= 0, lax.rem(rank + NX, NX) == home))
        def _():
            for i, ref in enumerate(outs):
                ref[0, 0] = source[i].astype(F32)


def expert_kernel(per, plan, place, got, weights, sent, *refs):
    outs, refs = refs[:NZ], refs[NZ:]
    pair, down, pair_sum, down_sum, back, kept, away, back_sem, grad_sem = refs
    x, own_z = place[0], place[1]
    count = plan[COUNT_AT, 0]
    for k in range(per):
        z = plan[Z_AT, k * NX + x]
        live = jnp.where(k * NX + x < count, 1.0, 0.0).astype(F32)
        for i in range(2):
            tile = weights[3 * z + i].astype(F32) * live
            pair[k, :, i * TILE : (i + 1) * TILE] = tile.astype(BF)
        down[k] = (weights[3 * z + 2].astype(F32) * live).astype(BF)
    pair_sum[...] = jnp.zeros_like(pair_sum)
    down_sum[...] = jnp.zeros_like(down_sum)
    group = 8
    rows = group * CAP
    tail = back_tail(per)
    ones = jnp.ones((ROWS, TILE), BF)

    def chunk(c, _):
        at = pl.ds(c * group, group)
        extra = got[at, 2 * CAP * per : 2 * CAP * per + AHEAD, :].astype(F32)
        slot = lax.broadcasted_iota(jnp.int32, (group, CAP, ROWS), 1).astype(F32)
        mine = extra[:, 1:2, :] == slot
        p = dot(jnp.where(mine, extra[:, 0:1, :], 0.0).reshape(rows, ROWS).astype(BF), ones)
        inner = jnp.zeros((rows, TILE), F32)
        pieces = []
        for k in range(per):
            both = got[at, 2 * CAP * k : 2 * CAP * (k + 1), :].astype(F32)
            rows_x = both[:, :CAP, :].reshape(rows, TILE).astype(BF)
            rows_dy = both[:, CAP:, :].reshape(rows, TILE)
            gu = dot(rows_x, pair[k])
            g, u = gu[:, :TILE], gu[:, TILE:]
            m = dot_nt(rows_dy.astype(BF), down[k])
            sig = jax.nn.sigmoid(g)
            act = g * sig
            h = (act * u).astype(BF)
            inner = inner + h.astype(F32) * m
            dh = p * m
            dg = (dh * u * sig * (1.0 + g * (1.0 - sig))).astype(BF)
            du = (dh * act).astype(BF)
            q = (p * rows_dy).astype(BF)
            dgu = jnp.concatenate([dg, du], axis=1)
            pieces.append(dot_nt(dgu, pair[k]).reshape(group, CAP, TILE))
            pair_sum[k] += dot_tn(rows_x, dgu)
            down_sum[k] += dot_tn(h, q)
        column = jnp.sum(inner, axis=1, keepdims=True).reshape(group, CAP, 1)
        row = jnp.sum(jnp.where(mine, column, 0.0), axis=1, keepdims=True)
        high = row.astype(BF).astype(F32)
        line = lax.broadcasted_iota(jnp.int32, (group, tail, ROWS), 1)
        pieces.append(jnp.where(line == 0, high, jnp.where(line == 1, row - high, 0.0)))
        back[at] = jnp.concatenate(pieces, axis=1).astype(BF)
        leave(c).start()
        return 0

    def leave(c):
        at = pl.ds(c * group, group)
        return pltpu.make_async_copy(back.at[at], sent.at[at], back_sem.at[c])

    def wait(c, _):
        leave(c).wait()
        return 0

    lax.fori_loop(0, PEERS // group, chunk, 0)
    kept[...] = jnp.zeros_like(kept)
    away[...] = jnp.zeros_like(away)
    for k in range(per):
        valid = k * NX + x < count
        shift = (plan[Z_AT, k * NX + x] - own_z) & (NZ - 1)

        @pl.when(jnp.logical_and(valid, shift == 0))
        def _():
            kept[0] = pair_sum[k, :, :TILE]
            kept[1] = pair_sum[k, :, TILE:]
            kept[2] = down_sum[k]

        @pl.when(jnp.logical_and(valid, shift > 0))
        def _():
            away[shift, 0] = pair_sum[k, :, :TILE].astype(BF)
            away[shift, 1] = pair_sum[k, :, TILE:].astype(BF)
            away[shift, 2] = down_sum[k].astype(BF)

    copies = [pltpu.make_async_copy(kept, outs[0], grad_sem.at[0])]
    for shift in range(1, NZ):
        copies.append(pltpu.make_async_copy(away.at[shift], outs[shift], grad_sem.at[shift]))
    for copy in copies:
        copy.start()
    for copy in copies:
        copy.wait()
    lax.fori_loop(0, PEERS // group, wait, 0)


def sum_kernel(own, *refs):
    total = own[...]
    for ref in refs[:-2]:
        total = total + ref[...].astype(F32)
    refs[-2][...] = total
    refs[-1][...] = total.astype(BF)


def combine_kernel(per, plans, ids, back, token_grad, prob_grad, parts, prob_rows):
    tail = back_tail(per)
    parts[...] = jnp.zeros_like(parts)

    def per_expert(e, _):
        rows = pl.ds(pl.multiple_of(e * CAP, 8), CAP)
        total = jnp.zeros((1, ROWS), F32)
        for x in range(NX):
            chunk = back[e * NX + x].astype(F32)
            for k in range(per):
                at = pl.multiple_of(plans[e, IN_AT, k * NX + x] * TILE, TILE)
                parts[rows, pl.ds(at, TILE)] += chunk[CAP * k : CAP * (k + 1), :]
            total = total + chunk[CAP * per : CAP * per + 1] + chunk[CAP * per + 1 : CAP * per + 2]
        prob_rows[pl.ds(e, 1), :] = total
        return 0

    lax.fori_loop(0, EXPERTS, per_expert, 0)
    first, second, place = assignment(ids[...])
    pick = one_hot(place)
    for j in range(WIDTH // 256):
        at = slice(j * 256, (j + 1) * 256)
        token_grad[:, at] = dot_tn(pick, parts[:, at].astype(BF)).astype(BF)
    rows = prob_rows[...]
    prob_grad[...] = jnp.concatenate(
        [
            jnp.sum(jnp.where(first, rows, 0.0), axis=0, keepdims=True),
            jnp.sum(jnp.where(second, rows, 0.0), axis=0, keepdims=True),
        ],
        axis=0,
    ).astype(BF)


def exchange(values, axes):
    return lax.all_to_all(values, axes, split_axis=0, concat_axis=0, tiled=True)


def moved(values, axis, shift):
    size = lax.axis_size(axis)
    return lax.ppermute(values, axis, [(i, (i + shift) % size) for i in range(size)])


def rest(per, plan, plans, place, ids, probs, tokens, cotangent, *sources):
    shape = jax.ShapeDtypeStruct
    triple = (3, TILE, TILE)
    ahead = 2 * CAP * per + AHEAD
    behind = CAP * per + back_tail(per)
    sent = call(
        functools.partial(dispatch_kernel, per),
        pltpu.HBM((PEERS, ahead, TILE), BF),
        [SMEM, VMEM, VMEM, VMEM, VMEM],
        HBM,
        [
            pltpu.VMEM((TOTAL, WIDTH), F32),
            pltpu.VMEM((TOTAL, WIDTH), F32),
            pltpu.VMEM((EXPERTS, ROWS), F32),
            pltpu.VMEM((EXPERTS, ROWS), F32),
            pltpu.VMEM((PEERS, ahead, TILE), BF),
            pltpu.SemaphoreType.DMA((EXPERTS,)),
        ],
    )(plans, ids, probs, tokens, cotangent)
    got = exchange(sent, ("expert", "x"))
    weights = call(
        pick_weights_kernel,
        shape(triple, BF),
        [SMEM, SMEM, VMEM, VMEM, VMEM, VMEM],
        VMEM,
    )(plan, place, *sources)
    weights = lax.all_gather(weights, "z", axis=0, tiled=True)
    back, *grads = call(
        functools.partial(expert_kernel, per),
        (
            pltpu.HBM((PEERS, behind, TILE), BF),
            pltpu.HBM(triple, F32),
            *[pltpu.HBM(triple, BF)] * (NZ - 1),
        ),
        [SMEM, SMEM, VMEM, VMEM],
        [HBM] * (NZ + 1),
        [
            pltpu.VMEM((per, TILE, 2 * TILE), BF),
            pltpu.VMEM((per, TILE, TILE), BF),
            pltpu.VMEM((per, TILE, 2 * TILE), F32),
            pltpu.VMEM((per, TILE, TILE), F32),
            pltpu.VMEM((PEERS, behind, TILE), BF),
            pltpu.VMEM(triple, F32),
            pltpu.VMEM((NZ,) + triple, BF),
            pltpu.SemaphoreType.DMA((PEERS // 8,)),
            pltpu.SemaphoreType.DMA((NZ,)),
        ],
    )(plan, place, got, weights)
    terms = [grads[0]] + [moved(grads[shift], "z", shift) for shift in (1, 7, 2, 6, 3, 5, 4)]
    returned = exchange(back, ("expert", "x"))
    own, sent = call(sum_kernel, (shape(triple, F32), shape(triple, BF)), [VMEM] * NZ, (VMEM, VMEM))(
        *terms
    )
    token_grad, prob_grad = call(
        functools.partial(combine_kernel, per),
        (shape((ROWS, WIDTH), BF), shape((2, ROWS), BF)),
        [SMEM, VMEM, VMEM],
        (VMEM, VMEM),
        [pltpu.VMEM((TOTAL, WIDTH), F32), pltpu.VMEM((EXPERTS, ROWS), F32)],
        pl.CostEstimate(
            flops=2 * ROWS * TOTAL * WIDTH,
            bytes_accessed=3 * 4 * TOTAL * WIDTH + 2 * PEERS * behind * TILE,
            transcendentals=0,
        ),
    )(plans, ids, returned)
    nearby = [moved(sent, "x", shift) for shift in range(1, NX)]
    token_grad, *nearby = lax.optimization_barrier((token_grad, *nearby))
    tile = shape((1, 1, TILE, TILE), F32)
    gate, up, down = call(
        pick_grads_kernel,
        (tile, tile, tile),
        [SMEM, SMEM, VMEM, VMEM, VMEM, VMEM],
        (VMEM, VMEM, VMEM),
    )(plan, place, own, *nearby)
    return token_grad, prob_grad, gate, up, down


def local(
    tokens,
    cotangent,
    expert_ids,
    probs,
    gate_tiles,
    up_tiles,
    down_tiles,
    in_ids,
    in_count,
    out_ids,
    out_count,
):
    shape = jax.ShapeDtypeStruct
    counts = jnp.concatenate([in_ids, in_count, out_ids, out_count], axis=0)
    plan, copies = call(
        plan_kernel,
        (shape((8, 128), jnp.int32), shape((EXPERTS, 8, 128), jnp.int32)),
        [VMEM],
        (VMEM, VMEM),
    )(counts)
    plans = exchange(copies, "expert")
    which = jnp.max(plans[:, BRANCH_AT, 0])
    place = jnp.stack([lax.axis_index("x"), lax.axis_index("z")]).astype(jnp.int32)
    ids = expert_ids.T
    rows = probs.T
    plan, *three = lax.optimization_barrier((plan, gate_tiles, up_tiles, down_tiles))
    own = jnp.concatenate([tile[0] for tile in three], axis=0)
    sources = [own] + [moved(own, "x", shift) for shift in range(1, NX)]
    token_grad, prob_grad, gate, up, down = lax.switch(
        which,
        [functools.partial(rest, size) for size in SIZES],
        plan,
        plans,
        place,
        ids,
        rows,
        tokens,
        cotangent,
        *sources,
    )
    return token_grad, prob_grad.T, gate, up, down


def solution(mesh):
    finer = Mesh(mesh.devices.reshape(EXPERTS, NX, NZ), ("expert", "x", "z"))
    rows = P(("expert", "x", "z"), None)
    tiles = P("expert", ("x", "z"), None, None)
    table = P("expert", None)
    return jax.shard_map(
        local,
        mesh=finer,
        in_specs=(rows, rows, rows, rows, tiles, tiles, tiles, table, table, table, table),
        out_specs=(rows, rows, tiles, tiles, tiles),
        check_vma=False,
    )
```

```python
import functools

import jax
import jax.numpy as jnp
from jax import lax
from jax.experimental import pallas as pl
from jax.experimental.pallas import tpu as pltpu
from jax.sharding import Mesh
from jax.sharding import PartitionSpec as P

FF = 8192
TILE = 128
COL_BLOCKS = FF // TILE
EXPERTS = 8
NX = 4
NZ = 8
SLOTS = NX * NZ
CAP = 40
ROWS = 128
WIDTH = 3072
TOTAL = EXPERTS * CAP
PEERS = EXPERTS * NX
AHEAD = 16
IN_AT, OUT_AT, Z_AT, COUNT_AT, RANK_AT, BRANCH_AT = range(6)
SIZES = (3, 4, 8)

BF = jnp.bfloat16
F32 = jnp.float32
SMEM = pl.BlockSpec(memory_space=pltpu.SMEM)
VMEM = pl.BlockSpec(memory_space=pltpu.VMEM)
HBM = pl.BlockSpec(memory_space=pltpu.HBM)
LIMIT = 40 * 1024 * 1024


def call(kernel, out, ins, outs, scratch=(), cost=None):
    return pl.pallas_call(
        kernel,
        out_shape=out,
        in_specs=ins,
        out_specs=outs,
        scratch_shapes=list(scratch),
        cost_estimate=cost,
        compiler_params=pltpu.CompilerParams(vmem_limit_bytes=LIMIT),
    )


def dot(a, b):
    return lax.dot_general(a, b, (((1,), (0,)), ((), ())), preferred_element_type=F32)


def dot_nt(a, b):
    return lax.dot_general(a, b, (((1,), (1,)), ((), ())), preferred_element_type=F32)


def dot_tn(a, b):
    return lax.dot_general(a, b, (((0,), (0,)), ((), ())), preferred_element_type=F32)


def lean(per):
    return per > 4


def block(j, size):
    if isinstance(j, int):
        return slice(j * size, (j + 1) * size)
    return pl.ds(pl.multiple_of(j * size, size), size)


def each(count, body, per):
    if lean(per):
        lax.fori_loop(0, count, lambda j, _: body(j) or 0, 0)
    else:
        for j in range(count):
            body(j)


def back_tail(per):
    return 16 if per % 2 == 0 else 8


def plan_kernel(counts, plan, copies):
    slot_i = lax.broadcasted_iota(jnp.int32, (SLOTS, SLOTS), 0)
    slot_j = lax.broadcasted_iota(jnp.int32, (SLOTS, SLOTS), 1)
    order_i = (slot_i & (NZ - 1)) * NX + (slot_i >> 3)
    order_j = (slot_j & (NZ - 1)) * NX + (slot_j >> 3)

    def column(line):
        return jnp.sum(jnp.where(slot_i == slot_j, line, 0.0), axis=1, keepdims=True)

    live = jnp.logical_and(counts[1:2, :] > 0, counts[3:4, :] > 0).astype(F32)
    rank = jnp.sum(jnp.where(order_j < order_i, live, 0.0), axis=1, keepdims=True)
    live_column = column(live)
    hot = jnp.logical_and(rank == slot_j.astype(F32), live_column > 0.0)

    def by_rank(values):
        return jnp.sum(jnp.where(hot, values, 0.0), axis=0, keepdims=True)

    rank_line = jnp.sum(jnp.where(order_i < order_j, live_column, 0.0), axis=0, keepdims=True)
    count = jnp.sum(live, axis=1, keepdims=True) + jnp.zeros_like(live)
    branch = jnp.zeros_like(live)
    for size in SIZES[:-1]:
        branch = branch + (count > NX * size).astype(F32)
    plan[...] = jnp.zeros_like(plan)
    for at, line in (
        (IN_AT, by_rank(column((counts[0:1, :] >> 6).astype(F32)))),
        (OUT_AT, by_rank(column(counts[2:3, :].astype(F32)))),
        (Z_AT, by_rank((slot_i & (NZ - 1)).astype(F32))),
        (COUNT_AT, count),
        (RANK_AT, jnp.where(live > 0.0, rank_line, -1.0)),
        (BRANCH_AT, branch),
    ):
        plan[at : at + 1, :SLOTS] = line.astype(jnp.int32)
    whole = plan[...]
    for e in range(EXPERTS):
        copies[e] = whole


def assignment(ids):
    experts = lax.broadcasted_iota(jnp.int32, (EXPERTS, ROWS), 0)
    first = ids[0:1, :] == experts
    second = ids[1:2, :] == experts
    named = jnp.logical_or(first, second)
    above = lax.broadcasted_iota(jnp.int32, (ROWS, ROWS), 0) < lax.broadcasted_iota(
        jnp.int32, (ROWS, ROWS), 1
    )
    place = dot(named.astype(F32).astype(BF), above.astype(F32).astype(BF))
    return first, second, jnp.where(named, place, -1.0)


def one_hot(place):
    at = lax.broadcasted_iota(jnp.int32, (CAP, ROWS), 0).astype(F32)
    rows = [(place[e : e + 1, :] == at).astype(F32) for e in range(EXPERTS)]
    return jnp.concatenate(rows, axis=0).astype(BF)


def dispatch_kernel(per, plans, ids, probs, tokens, cot, sent, xs, ys, prob_rows, places, out, sem):
    first, second, place = assignment(ids[...])
    p = probs[...].astype(F32)
    prob_rows[...] = jnp.where(first, p[0:1, :], 0.0) + jnp.where(second, p[1:2, :], 0.0)
    places[...] = place
    pick = one_hot(place)

    def gather(j):
        at = block(j, 256)
        xs[:, at] = dot(pick, tokens[:, at])
        ys[:, at] = dot(pick, cot[:, at])

    each(WIDTH // 256, gather, per)
    line = lax.broadcasted_iota(jnp.int32, (AHEAD, ROWS), 0)

    def per_expert(e, _):
        rows = pl.ds(pl.multiple_of(e * CAP, 8), CAP)
        extra = jnp.where(
            line == 0,
            prob_rows[pl.ds(e, 1), :],
            jnp.where(line == 1, places[pl.ds(e, 1), :], 0.0),
        ).astype(BF)
        for x in range(NX):
            for k in range(per):
                r = k * NX + x
                at_in = pl.multiple_of(plans[e, IN_AT, r] * TILE, TILE)
                at_out = pl.multiple_of(plans[e, OUT_AT, r] * TILE, TILE)
                both = jnp.concatenate(
                    [xs[rows, pl.ds(at_in, TILE)], ys[rows, pl.ds(at_out, TILE)]], axis=0
                )
                out[e * NX + x, 2 * CAP * k : 2 * CAP * (k + 1), :] = both.astype(BF)
            out[e * NX + x, 2 * CAP * per : 2 * CAP * per + AHEAD, :] = extra
        leave(e).start()
        return 0

    def leave(e):
        part = pl.ds(e * NX, NX)
        return pltpu.make_async_copy(out.at[part], sent.at[part], sem.at[e])

    def wait(e, _):
        leave(e).wait()
        return 0

    lax.fori_loop(0, EXPERTS, per_expert, 0)
    lax.fori_loop(0, EXPERTS, wait, 0)


def pick_weights_kernel(plan, place, own, one, two, three, out):
    x, z = place[0], place[1]
    out[...] = jnp.zeros_like(out)
    for shift, source in enumerate((own, one, two, three)):
        home = lax.rem(x + NX - shift, NX)
        rank = plan[RANK_AT, home * NZ + z]

        @pl.when(jnp.logical_and(rank >= 0, lax.rem(rank + NX, NX) == x))
        def _():
            out[...] = source[...]


def pick_grads_kernel(plan, place, own, one, two, three, gate, up, down):
    x, z = place[0], place[1]
    rank = plan[RANK_AT, x * NZ + z]
    outs = (gate, up, down)
    for ref in outs:
        ref[...] = jnp.zeros_like(ref)
    for shift, source in enumerate((own, one, two, three)):
        home = lax.rem(x + NX - shift, NX)

        @pl.when(jnp.logical_and(rank >= 0, lax.rem(rank + NX, NX) == home))
        def _():
            for i, ref in enumerate(outs):
                ref[0, 0] = source[i].astype(F32)


def expert_kernel(per, plan, place, got, weights, sent, *refs):
    outs, refs = refs[:NZ], refs[NZ:]
    pair, down, pair_sum, down_sum, back, kept, away, back_sem, grad_sem = refs
    x, own_z = place[0], place[1]
    count = plan[COUNT_AT, 0]
    for k in range(per):
        z = plan[Z_AT, k * NX + x]
        live = jnp.where(k * NX + x < count, 1.0, 0.0).astype(F32)
        for i in range(2):
            tile = weights[3 * z + i].astype(F32) * live
            pair[k, :, i * TILE : (i + 1) * TILE] = tile.astype(BF)
        down[k] = (weights[3 * z + 2].astype(F32) * live).astype(BF)
    pair_sum[...] = jnp.zeros_like(pair_sum)
    down_sum[...] = jnp.zeros_like(down_sum)
    group = 8
    rows = group * CAP
    tail = back_tail(per)
    ones = jnp.ones((ROWS, TILE), BF)

    def chunk(c, _):
        at = pl.ds(c * group, group)
        extra = got[at, 2 * CAP * per : 2 * CAP * per + AHEAD, :].astype(F32)
        slot = lax.broadcasted_iota(jnp.int32, (group, CAP, ROWS), 1).astype(F32)
        mine = extra[:, 1:2, :] == slot
        p = dot(jnp.where(mine, extra[:, 0:1, :], 0.0).reshape(rows, ROWS).astype(BF), ones)
        inner = jnp.zeros((rows, TILE), F32)
        pieces = []
        for k in range(per):
            both = got[at, 2 * CAP * k : 2 * CAP * (k + 1), :].astype(F32)
            rows_x = both[:, :CAP, :].reshape(rows, TILE).astype(BF)
            rows_dy = both[:, CAP:, :].reshape(rows, TILE)
            gu = dot(rows_x, pair[k])
            g, u = gu[:, :TILE], gu[:, TILE:]
            m = dot_nt(rows_dy.astype(BF), down[k])
            sig = jax.nn.sigmoid(g)
            act = g * sig
            h = (act * u).astype(BF)
            inner = inner + h.astype(F32) * m
            dh = p * m
            dg = (dh * u * sig * (1.0 + g * (1.0 - sig))).astype(BF)
            du = (dh * act).astype(BF)
            q = (p * rows_dy).astype(BF)
            dgu = jnp.concatenate([dg, du], axis=1)
            pieces.append(dot_nt(dgu, pair[k]).reshape(group, CAP, TILE))
            pair_sum[k] += dot_tn(rows_x, dgu)
            down_sum[k] += dot_tn(h, q)
        column = jnp.sum(inner, axis=1, keepdims=True).reshape(group, CAP, 1)
        row = jnp.sum(jnp.where(mine, column, 0.0), axis=1, keepdims=True)
        high = row.astype(BF).astype(F32)
        line = lax.broadcasted_iota(jnp.int32, (group, tail, ROWS), 1)
        pieces.append(jnp.where(line == 0, high, jnp.where(line == 1, row - high, 0.0)))
        back[at] = jnp.concatenate(pieces, axis=1).astype(BF)
        leave(c).start()
        return 0

    def leave(c):
        at = pl.ds(c * group, group)
        return pltpu.make_async_copy(back.at[at], sent.at[at], back_sem.at[c])

    def wait(c, _):
        leave(c).wait()
        return 0

    lax.fori_loop(0, PEERS // group, chunk, 0)
    kept[...] = jnp.zeros_like(kept)
    away[...] = jnp.zeros_like(away)
    for k in range(per):
        valid = k * NX + x < count
        shift = (plan[Z_AT, k * NX + x] - own_z) & (NZ - 1)

        @pl.when(jnp.logical_and(valid, shift == 0))
        def _():
            kept[0] = pair_sum[k, :, :TILE]
            kept[1] = pair_sum[k, :, TILE:]
            kept[2] = down_sum[k]

        @pl.when(jnp.logical_and(valid, shift > 0))
        def _():
            away[shift, 0] = pair_sum[k, :, :TILE].astype(BF)
            away[shift, 1] = pair_sum[k, :, TILE:].astype(BF)
            away[shift, 2] = down_sum[k].astype(BF)

    copies = [pltpu.make_async_copy(kept, outs[0], grad_sem.at[0])]
    for shift in range(1, NZ):
        copies.append(pltpu.make_async_copy(away.at[shift], outs[shift], grad_sem.at[shift]))
    for copy in copies:
        copy.start()
    for copy in copies:
        copy.wait()
    lax.fori_loop(0, PEERS // group, wait, 0)


def sum_kernel(own, *refs):
    total = own[...]
    for ref in refs[:-2]:
        total = total + ref[...].astype(F32)
    refs[-2][...] = total
    refs[-1][...] = total.astype(BF)


def combine_kernel(per, plans, ids, back, token_grad, prob_grad, parts, prob_rows):
    tail = back_tail(per)
    parts[...] = jnp.zeros_like(parts)

    def per_expert(e, _):
        rows = pl.ds(pl.multiple_of(e * CAP, 8), CAP)
        total = jnp.zeros((1, ROWS), F32)
        for x in range(NX):
            chunk = back[e * NX + x].astype(F32)
            for k in range(per):
                at = pl.multiple_of(plans[e, IN_AT, k * NX + x] * TILE, TILE)
                parts[rows, pl.ds(at, TILE)] += chunk[CAP * k : CAP * (k + 1), :]
            total = total + chunk[CAP * per : CAP * per + 1] + chunk[CAP * per + 1 : CAP * per + 2]
        prob_rows[pl.ds(e, 1), :] = total
        return 0

    lax.fori_loop(0, EXPERTS, per_expert, 0)
    first, second, place = assignment(ids[...])
    pick = one_hot(place)

    def gather(j):
        at = block(j, 256)
        token_grad[:, at] = dot_tn(pick, parts[:, at].astype(BF)).astype(BF)

    each(WIDTH // 256, gather, per)
    rows = prob_rows[...]
    prob_grad[...] = jnp.concatenate(
        [
            jnp.sum(jnp.where(first, rows, 0.0), axis=0, keepdims=True),
            jnp.sum(jnp.where(second, rows, 0.0), axis=0, keepdims=True),
        ],
        axis=0,
    ).astype(BF)


def exchange(values, axes):
    return lax.all_to_all(values, axes, split_axis=0, concat_axis=0, tiled=True)


def moved(values, axis, shift):
    size = lax.axis_size(axis)
    return lax.ppermute(values, axis, [(i, (i + shift) % size) for i in range(size)])


def rest(per, plan, plans, place, ids, probs, tokens, cotangent, *sources):
    shape = jax.ShapeDtypeStruct
    triple = (3, TILE, TILE)
    ahead = 2 * CAP * per + AHEAD
    behind = CAP * per + back_tail(per)
    sent = call(
        functools.partial(dispatch_kernel, per),
        pltpu.HBM((PEERS, ahead, TILE), BF),
        [SMEM, VMEM, VMEM, VMEM, VMEM],
        HBM,
        [
            pltpu.VMEM((TOTAL, WIDTH), F32),
            pltpu.VMEM((TOTAL, WIDTH), F32),
            pltpu.VMEM((EXPERTS, ROWS), F32),
            pltpu.VMEM((EXPERTS, ROWS), F32),
            pltpu.VMEM((PEERS, ahead, TILE), BF),
            pltpu.SemaphoreType.DMA((EXPERTS,)),
        ],
    )(plans, ids, probs, tokens, cotangent)
    got = exchange(sent, ("expert", "x"))
    weights = call(
        pick_weights_kernel,
        shape(triple, BF),
        [SMEM, SMEM, VMEM, VMEM, VMEM, VMEM],
        VMEM,
    )(plan, place, *sources)
    weights = lax.all_gather(weights, "z", axis=0, tiled=True)
    back, *grads = call(
        functools.partial(expert_kernel, per),
        (
            pltpu.HBM((PEERS, behind, TILE), BF),
            pltpu.HBM(triple, F32),
            *[pltpu.HBM(triple, BF)] * (NZ - 1),
        ),
        [SMEM, SMEM, VMEM, VMEM],
        [HBM] * (NZ + 1),
        [
            pltpu.VMEM((per, TILE, 2 * TILE), BF),
            pltpu.VMEM((per, TILE, TILE), BF),
            pltpu.VMEM((per, TILE, 2 * TILE), F32),
            pltpu.VMEM((per, TILE, TILE), F32),
            pltpu.VMEM((PEERS, behind, TILE), BF),
            pltpu.VMEM(triple, F32),
            pltpu.VMEM((NZ,) + triple, BF),
            pltpu.SemaphoreType.DMA((PEERS // 8,)),
            pltpu.SemaphoreType.DMA((NZ,)),
        ],
    )(plan, place, got, weights)
    returned = exchange(back, ("expert", "x"))
    if lean(per):
        ordered = jnp.roll(jnp.stack([term.astype(F32) for term in grads]), place[1], axis=0)
        own = jnp.sum(exchange(ordered, "z"), axis=0)
        whole = exchange(jnp.broadcast_to(own[None], (NX,) + triple), "x")
        nearby = [
            lax.dynamic_index_in_dim(whole, (place[0] + NX - shift) % NX, keepdims=False)
            for shift in range(1, NX)
        ]
    else:
        terms = [moved(grads[shift], "z", shift) for shift in (1, 7, 2, 6, 3, 5, 4)]
        own, sent = call(
            sum_kernel, (shape(triple, F32), shape(triple, BF)), [VMEM] * NZ, (VMEM, VMEM)
        )(grads[0], *terms)
        nearby = [moved(sent, "x", shift) for shift in range(1, NX)]
    token_grad, prob_grad = call(
        functools.partial(combine_kernel, per),
        (shape((ROWS, WIDTH), BF), shape((2, ROWS), BF)),
        [SMEM, VMEM, VMEM],
        (VMEM, VMEM),
        [pltpu.VMEM((TOTAL, WIDTH), F32), pltpu.VMEM((EXPERTS, ROWS), F32)],
        pl.CostEstimate(
            flops=2 * ROWS * TOTAL * WIDTH,
            bytes_accessed=3 * 4 * TOTAL * WIDTH + 2 * PEERS * behind * TILE,
            transcendentals=0,
        ),
    )(plans, ids, returned)
    token_grad, *nearby = lax.optimization_barrier((token_grad, *nearby))
    tile = shape((1, 1, TILE, TILE), F32)
    gate, up, down = call(
        pick_grads_kernel,
        (tile, tile, tile),
        [SMEM, SMEM, VMEM, VMEM, VMEM, VMEM],
        (VMEM, VMEM, VMEM),
    )(plan, place, own, *nearby)
    return token_grad, prob_grad, gate, up, down


def local(
    tokens,
    cotangent,
    expert_ids,
    probs,
    gate_tiles,
    up_tiles,
    down_tiles,
    in_ids,
    in_count,
    out_ids,
    out_count,
):
    shape = jax.ShapeDtypeStruct
    counts = jnp.concatenate([in_ids, in_count, out_ids, out_count], axis=0)
    plan, copies = call(
        plan_kernel,
        (shape((8, 128), jnp.int32), shape((EXPERTS, 8, 128), jnp.int32)),
        [VMEM],
        (VMEM, VMEM),
    )(counts)
    plans = exchange(copies, "expert")
    which = jnp.max(plans[:, BRANCH_AT, 0])
    place = jnp.stack([lax.axis_index("x"), lax.axis_index("z")]).astype(jnp.int32)
    ids = expert_ids.T
    rows = probs.T
    plan, *three = lax.optimization_barrier((plan, gate_tiles, up_tiles, down_tiles))
    own = jnp.concatenate([tile[0] for tile in three], axis=0)
    sources = [own] + [moved(own, "x", shift) for shift in range(1, NX)]
    token_grad, prob_grad, gate, up, down = lax.switch(
        which,
        [functools.partial(rest, size) for size in SIZES],
        plan,
        plans,
        place,
        ids,
        rows,
        tokens,
        cotangent,
        *sources,
    )
    return token_grad, prob_grad.T, gate, up, down


def solution(mesh):
    finer = Mesh(mesh.devices.reshape(EXPERTS, NX, NZ), ("expert", "x", "z"))
    rows = P(("expert", "x", "z"), None)
    tiles = P("expert", ("x", "z"), None, None)
    table = P("expert", None)
    return jax.shard_map(
        local,
        mesh=finer,
        in_specs=(rows, rows, rows, rows, tiles, tiles, tiles, table, table, table, table),
        out_specs=(rows, rows, tiles, tiles, tiles),
        check_vma=False,
    )
```

```python
import functools

import jax
import jax.numpy as jnp
from jax import lax
from jax.experimental import pallas as pl
from jax.experimental.pallas import tpu as pltpu
from jax.sharding import Mesh
from jax.sharding import PartitionSpec as P

FF = 8192
TILE = 128
COL_BLOCKS = FF // TILE
EXPERTS = 8
NX = 4
NZ = 8
SLOTS = NX * NZ
CAP = 40
ROWS = 128
WIDTH = 3072
TOTAL = EXPERTS * CAP
PEERS = EXPERTS * NX
AHEAD = 16
IN_AT, OUT_AT, Z_AT, COUNT_AT, RANK_AT, BRANCH_AT = range(6)
SIZES = (3, 4, 8)
CHUNKS = (1, 4, 7, 5, 2, 3, 6)
WAVES = ((0, 2), (2, 2), (4, 1), (5, 2))

BF = jnp.bfloat16
F32 = jnp.float32
SMEM = pl.BlockSpec(memory_space=pltpu.SMEM)
VMEM = pl.BlockSpec(memory_space=pltpu.VMEM)
HBM = pl.BlockSpec(memory_space=pltpu.HBM)
LIMIT = 40 * 1024 * 1024


def call(kernel, out, ins, outs, scratch=(), cost=None):
    return pl.pallas_call(
        kernel,
        out_shape=out,
        in_specs=ins,
        out_specs=outs,
        scratch_shapes=list(scratch),
        cost_estimate=cost,
        compiler_params=pltpu.CompilerParams(vmem_limit_bytes=LIMIT),
    )


def dot(a, b):
    return lax.dot_general(a, b, (((1,), (0,)), ((), ())), preferred_element_type=F32)


def dot_nt(a, b):
    return lax.dot_general(a, b, (((1,), (1,)), ((), ())), preferred_element_type=F32)


def dot_tn(a, b):
    return lax.dot_general(a, b, (((0,), (0,)), ((), ())), preferred_element_type=F32)


def lean(per):
    return per > 4


def block(j, size):
    if isinstance(j, int):
        return slice(j * size, (j + 1) * size)
    return pl.ds(pl.multiple_of(j * size, size), size)


def each(count, body, per):
    if lean(per):
        lax.fori_loop(0, count, lambda j, _: body(j) or 0, 0)
    else:
        for j in range(count):
            body(j)


def back_tail(per):
    return 16 if per % 2 == 0 else 8


def plan_kernel(counts, plan, copies):
    slot_i = lax.broadcasted_iota(jnp.int32, (SLOTS, SLOTS), 0)
    slot_j = lax.broadcasted_iota(jnp.int32, (SLOTS, SLOTS), 1)
    order_i = (slot_i & (NZ - 1)) * NX + (slot_i >> 3)
    order_j = (slot_j & (NZ - 1)) * NX + (slot_j >> 3)

    def column(line):
        return jnp.sum(jnp.where(slot_i == slot_j, line, 0.0), axis=1, keepdims=True)

    live = jnp.logical_and(counts[1:2, :] > 0, counts[3:4, :] > 0).astype(F32)
    rank = jnp.sum(jnp.where(order_j < order_i, live, 0.0), axis=1, keepdims=True)
    live_column = column(live)
    hot = jnp.logical_and(rank == slot_j.astype(F32), live_column > 0.0)

    def by_rank(values):
        return jnp.sum(jnp.where(hot, values, 0.0), axis=0, keepdims=True)

    rank_line = jnp.sum(jnp.where(order_i < order_j, live_column, 0.0), axis=0, keepdims=True)
    count = jnp.sum(live, axis=1, keepdims=True) + jnp.zeros_like(live)
    branch = jnp.zeros_like(live)
    for size in SIZES[:-1]:
        branch = branch + (count > NX * size).astype(F32)
    plan[...] = jnp.zeros_like(plan)
    for at, line in (
        (IN_AT, by_rank(column((counts[0:1, :] >> 6).astype(F32)))),
        (OUT_AT, by_rank(column(counts[2:3, :].astype(F32)))),
        (Z_AT, by_rank((slot_i & (NZ - 1)).astype(F32))),
        (COUNT_AT, count),
        (RANK_AT, jnp.where(live > 0.0, rank_line, -1.0)),
        (BRANCH_AT, branch),
    ):
        plan[at : at + 1, :SLOTS] = line.astype(jnp.int32)
    whole = plan[...]
    for e in range(EXPERTS):
        copies[e] = whole


def assignment(ids):
    experts = lax.broadcasted_iota(jnp.int32, (EXPERTS, ROWS), 0)
    first = ids[0:1, :] == experts
    second = ids[1:2, :] == experts
    named = jnp.logical_or(first, second)
    above = lax.broadcasted_iota(jnp.int32, (ROWS, ROWS), 0) < lax.broadcasted_iota(
        jnp.int32, (ROWS, ROWS), 1
    )
    place = dot(named.astype(F32).astype(BF), above.astype(F32).astype(BF))
    return first, second, jnp.where(named, place, -1.0)


def one_hot(place):
    at = lax.broadcasted_iota(jnp.int32, (CAP, ROWS), 0).astype(F32)
    rows = [(place[e : e + 1, :] == at).astype(F32) for e in range(EXPERTS)]
    return jnp.concatenate(rows, axis=0).astype(BF)


def dispatch_kernel(per, plans, ids, probs, tokens, cot, sent, xs, ys, prob_rows, places, out, sem):
    first, second, place = assignment(ids[...])
    p = probs[...].astype(F32)
    prob_rows[...] = jnp.where(first, p[0:1, :], 0.0) + jnp.where(second, p[1:2, :], 0.0)
    places[...] = place
    pick = one_hot(place)

    def gather(j):
        at = block(j, 256)
        xs[:, at] = dot(pick, tokens[:, at])
        ys[:, at] = dot(pick, cot[:, at])

    each(WIDTH // 256, gather, per)
    line = lax.broadcasted_iota(jnp.int32, (AHEAD, ROWS), 0)

    def per_expert(e, _):
        rows = pl.ds(pl.multiple_of(e * CAP, 8), CAP)
        extra = jnp.where(
            line == 0,
            prob_rows[pl.ds(e, 1), :],
            jnp.where(line == 1, places[pl.ds(e, 1), :], 0.0),
        ).astype(BF)
        for x in range(NX):
            for k in range(per):
                r = k * NX + x
                at_in = pl.multiple_of(plans[e, IN_AT, r] * TILE, TILE)
                at_out = pl.multiple_of(plans[e, OUT_AT, r] * TILE, TILE)
                both = jnp.concatenate(
                    [xs[rows, pl.ds(at_in, TILE)], ys[rows, pl.ds(at_out, TILE)]], axis=0
                )
                out[e * NX + x, 2 * CAP * k : 2 * CAP * (k + 1), :] = both.astype(BF)
            out[e * NX + x, 2 * CAP * per : 2 * CAP * per + AHEAD, :] = extra
        leave(e).start()
        return 0

    def leave(e):
        part = pl.ds(e * NX, NX)
        return pltpu.make_async_copy(out.at[part], sent.at[part], sem.at[e])

    def wait(e, _):
        leave(e).wait()
        return 0

    lax.fori_loop(0, EXPERTS, per_expert, 0)
    lax.fori_loop(0, EXPERTS, wait, 0)


def pick_weights_kernel(plan, place, own, one, two, three, out):
    x, z = place[0], place[1]
    out[...] = jnp.zeros_like(out)
    for shift, source in enumerate((own, one, two, three)):
        home = lax.rem(x + NX - shift, NX)
        rank = plan[RANK_AT, home * NZ + z]

        @pl.when(jnp.logical_and(rank >= 0, lax.rem(rank + NX, NX) == x))
        def _():
            out[...] = source[...]


def pick_grads_kernel(plan, place, own, one, two, three, gate, up, down):
    x, z = place[0], place[1]
    rank = plan[RANK_AT, x * NZ + z]
    outs = (gate, up, down)
    for ref in outs:
        ref[...] = jnp.zeros_like(ref)
    for shift, source in enumerate((own, one, two, three)):
        home = lax.rem(x + NX - shift, NX)

        @pl.when(jnp.logical_and(rank >= 0, lax.rem(rank + NX, NX) == home))
        def _():
            for i, ref in enumerate(outs):
                ref[0, 0] = source[i].astype(F32)


def expert_kernel(per, plan, place, got, weights, sent, *refs):
    outs, refs = refs[: len(WAVES) + 1], refs[len(WAVES) + 1 :]
    pair, down, pair_sum, down_sum, back, kept, away, back_sem, grad_sem = refs
    x, own_z = place[0], place[1]
    count = plan[COUNT_AT, 0]
    for k in range(per):
        z = plan[Z_AT, k * NX + x]
        live = jnp.where(k * NX + x < count, 1.0, 0.0).astype(F32)
        for i in range(2):
            tile = weights[3 * z + i].astype(F32) * live
            pair[k, :, i * TILE : (i + 1) * TILE] = tile.astype(BF)
        down[k] = (weights[3 * z + 2].astype(F32) * live).astype(BF)
    pair_sum[...] = jnp.zeros_like(pair_sum)
    down_sum[...] = jnp.zeros_like(down_sum)
    group = 8
    rows = group * CAP
    tail = back_tail(per)
    ones = jnp.ones((ROWS, TILE), BF)

    def chunk(c, _):
        at = pl.ds(c * group, group)
        extra = got[at, 2 * CAP * per : 2 * CAP * per + AHEAD, :].astype(F32)
        slot = lax.broadcasted_iota(jnp.int32, (group, CAP, ROWS), 1).astype(F32)
        mine = extra[:, 1:2, :] == slot
        p = dot(jnp.where(mine, extra[:, 0:1, :], 0.0).reshape(rows, ROWS).astype(BF), ones)
        inner = jnp.zeros((rows, TILE), F32)
        pieces = []
        for k in range(per):
            both = got[at, 2 * CAP * k : 2 * CAP * (k + 1), :].astype(F32)
            rows_x = both[:, :CAP, :].reshape(rows, TILE).astype(BF)
            rows_dy = both[:, CAP:, :].reshape(rows, TILE)
            gu = dot(rows_x, pair[k])
            g, u = gu[:, :TILE], gu[:, TILE:]
            m = dot_nt(rows_dy.astype(BF), down[k])
            sig = jax.nn.sigmoid(g)
            act = g * sig
            h = (act * u).astype(BF)
            inner = inner + h.astype(F32) * m
            dh = p * m
            dg = (dh * u * sig * (1.0 + g * (1.0 - sig))).astype(BF)
            du = (dh * act).astype(BF)
            q = (p * rows_dy).astype(BF)
            dgu = jnp.concatenate([dg, du], axis=1)
            pieces.append(dot_nt(dgu, pair[k]).reshape(group, CAP, TILE))
            pair_sum[k] += dot_tn(rows_x, dgu)
            down_sum[k] += dot_tn(h, q)
        column = jnp.sum(inner, axis=1, keepdims=True).reshape(group, CAP, 1)
        row = jnp.sum(jnp.where(mine, column, 0.0), axis=1, keepdims=True)
        high = row.astype(BF).astype(F32)
        line = lax.broadcasted_iota(jnp.int32, (group, tail, ROWS), 1)
        pieces.append(jnp.where(line == 0, high, jnp.where(line == 1, row - high, 0.0)))
        back[at] = jnp.concatenate(pieces, axis=1).astype(BF)
        leave(c).start()
        return 0

    def leave(c):
        at = pl.ds(c * group, group)
        return pltpu.make_async_copy(back.at[at], sent.at[at], back_sem.at[c])

    def wait(c, _):
        leave(c).wait()
        return 0

    lax.fori_loop(0, PEERS // group, chunk, 0)
    kept[...] = jnp.zeros_like(kept)
    away[...] = jnp.zeros_like(away)
    for k in range(per):
        valid = k * NX + x < count
        shift = (plan[Z_AT, k * NX + x] - own_z) & (NZ - 1)

        away_from_here = shift > 0

        @pl.when(jnp.logical_and(valid, shift == 0))
        def _():
            kept[0] = pair_sum[k, :, :TILE]
            kept[1] = pair_sum[k, :, TILE:]
            kept[2] = down_sum[k]

        shift = sum(jnp.where(shift == s, i, 0) for i, s in enumerate(CHUNKS))

        @pl.when(jnp.logical_and(valid, away_from_here))
        def _():
            away[shift, 0] = pair_sum[k, :, :TILE].astype(BF)
            away[shift, 1] = pair_sum[k, :, TILE:].astype(BF)
            away[shift, 2] = down_sum[k].astype(BF)

    copies = [pltpu.make_async_copy(kept, outs[0], grad_sem.at[0])]
    for i, (start, size) in enumerate(WAVES):
        part = away.at[start : start + size]
        copies.append(pltpu.make_async_copy(part, outs[i + 1], grad_sem.at[i + 1]))
    for copy in copies:
        copy.start()
    for copy in copies:
        copy.wait()
    lax.fori_loop(0, PEERS // group, wait, 0)


def relay_kernel(stay, below, above, up, down):
    up[...] = (stay[0].astype(F32) + below[1].astype(F32)).astype(BF)
    down[...] = (stay[1].astype(F32) + above[1].astype(F32)).astype(BF)


def sum_kernel(own, below, above, *refs):
    total = own[...] + below[0].astype(F32) + above[0].astype(F32)
    for ref in refs[:-2]:
        total = total + ref[...].reshape(total.shape).astype(F32)
    refs[-2][...] = total
    refs[-1][...] = total.astype(BF)


def combine_kernel(per, plans, ids, back, token_grad, prob_grad, parts, prob_rows):
    tail = back_tail(per)
    parts[...] = jnp.zeros_like(parts)

    def per_expert(e, _):
        rows = pl.ds(pl.multiple_of(e * CAP, 8), CAP)
        total = jnp.zeros((1, ROWS), F32)
        for x in range(NX):
            chunk = back[e * NX + x].astype(F32)
            for k in range(per):
                at = pl.multiple_of(plans[e, IN_AT, k * NX + x] * TILE, TILE)
                parts[rows, pl.ds(at, TILE)] += chunk[CAP * k : CAP * (k + 1), :]
            total = total + chunk[CAP * per : CAP * per + 1] + chunk[CAP * per + 1 : CAP * per + 2]
        prob_rows[pl.ds(e, 1), :] = total
        return 0

    lax.fori_loop(0, EXPERTS, per_expert, 0)
    first, second, place = assignment(ids[...])
    pick = one_hot(place)

    def gather(j):
        at = block(j, 256)
        token_grad[:, at] = dot_tn(pick, parts[:, at].astype(BF)).astype(BF)

    each(WIDTH // 256, gather, per)
    rows = prob_rows[...]
    prob_grad[...] = jnp.concatenate(
        [
            jnp.sum(jnp.where(first, rows, 0.0), axis=0, keepdims=True),
            jnp.sum(jnp.where(second, rows, 0.0), axis=0, keepdims=True),
        ],
        axis=0,
    ).astype(BF)


def exchange(values, axes):
    return lax.all_to_all(values, axes, split_axis=0, concat_axis=0, tiled=True)


def moved(values, axis, shift):
    size = lax.axis_size(axis)
    return lax.ppermute(values, axis, [(i, (i + shift) % size) for i in range(size)])


def rest(per, plan, plans, place, ids, probs, tokens, cotangent, *sources):
    shape = jax.ShapeDtypeStruct
    triple = (3, TILE, TILE)
    ahead = 2 * CAP * per + AHEAD
    behind = CAP * per + back_tail(per)
    sent = call(
        functools.partial(dispatch_kernel, per),
        pltpu.HBM((PEERS, ahead, TILE), BF),
        [SMEM, VMEM, VMEM, VMEM, VMEM],
        HBM,
        [
            pltpu.VMEM((TOTAL, WIDTH), F32),
            pltpu.VMEM((TOTAL, WIDTH), F32),
            pltpu.VMEM((EXPERTS, ROWS), F32),
            pltpu.VMEM((EXPERTS, ROWS), F32),
            pltpu.VMEM((PEERS, ahead, TILE), BF),
            pltpu.SemaphoreType.DMA((EXPERTS,)),
        ],
    )(plans, ids, probs, tokens, cotangent)
    got = exchange(sent, ("expert", "x"))
    weights = call(
        pick_weights_kernel,
        shape(triple, BF),
        [SMEM, SMEM, VMEM, VMEM, VMEM, VMEM],
        VMEM,
    )(plan, place, *sources)
    weights = lax.all_gather(weights, "z", axis=0, tiled=True)
    back, *grads = call(
        functools.partial(expert_kernel, per),
        (
            pltpu.HBM((PEERS, behind, TILE), BF),
            pltpu.HBM(triple, F32),
            *[pltpu.HBM((size,) + triple, BF) for _, size in WAVES],
        ),
        [SMEM, SMEM, VMEM, VMEM],
        [HBM] * (len(WAVES) + 2),
        [
            pltpu.VMEM((per, TILE, 2 * TILE), BF),
            pltpu.VMEM((per, TILE, TILE), BF),
            pltpu.VMEM((per, TILE, 2 * TILE), F32),
            pltpu.VMEM((per, TILE, TILE), F32),
            pltpu.VMEM((PEERS, behind, TILE), BF),
            pltpu.VMEM(triple, F32),
            pltpu.VMEM((NZ - 1,) + triple, BF),
            pltpu.SemaphoreType.DMA((PEERS // 8,)),
            pltpu.SemaphoreType.DMA((len(WAVES) + 1,)),
        ],
    )(plan, place, got, weights)
    returned = exchange(back, ("expert", "x"))
    if lean(per):
        chunks = jnp.concatenate(grads[1:], axis=0)
        chunks = [grads[0]] + [chunks[CHUNKS.index(shift)].astype(F32) for shift in range(1, NZ)]
        ordered = jnp.roll(jnp.stack(chunks), place[1], axis=0)
        own = jnp.sum(exchange(ordered, "z"), axis=0)
        whole = exchange(jnp.broadcast_to(own[None], (NX,) + triple), "x")
        nearby = [
            lax.dynamic_index_in_dim(whole, (place[0] + NX - shift) % NX, keepdims=False)
            for shift in range(1, NX)
        ]
    else:
        kept, plus_one, minus_one, plus_two, stay = grads
        below, above = moved(plus_one, "z", 1), moved(minus_one, "z", NZ - 1)
        two = moved(plus_two, "z", 2)
        up, down = call(relay_kernel, (shape(triple, BF),) * 2, [VMEM] * 3, (VMEM, VMEM))(
            stay, below, above
        )
        own, sent = call(
            sum_kernel, (shape(triple, F32), shape(triple, BF)), [VMEM] * 6, (VMEM, VMEM)
        )(kept, below, above, two, moved(up, "z", 3), moved(down, "z", NZ - 2))
        nearby = [moved(sent, "x", shift) for shift in range(1, NX)]
    token_grad, prob_grad = call(
        functools.partial(combine_kernel, per),
        (shape((ROWS, WIDTH), BF), shape((2, ROWS), BF)),
        [SMEM, VMEM, VMEM],
        (VMEM, VMEM),
        [pltpu.VMEM((TOTAL, WIDTH), F32), pltpu.VMEM((EXPERTS, ROWS), F32)],
        pl.CostEstimate(
            flops=2 * ROWS * TOTAL * WIDTH,
            bytes_accessed=3 * 4 * TOTAL * WIDTH + 2 * PEERS * behind * TILE,
            transcendentals=0,
        ),
    )(plans, ids, returned)
    token_grad, *nearby = lax.optimization_barrier((token_grad, *nearby))
    tile = shape((1, 1, TILE, TILE), F32)
    gate, up, down = call(
        pick_grads_kernel,
        (tile, tile, tile),
        [SMEM, SMEM, VMEM, VMEM, VMEM, VMEM],
        (VMEM, VMEM, VMEM),
    )(plan, place, own, *nearby)
    return token_grad, prob_grad, gate, up, down


def local(
    tokens,
    cotangent,
    expert_ids,
    probs,
    gate_tiles,
    up_tiles,
    down_tiles,
    in_ids,
    in_count,
    out_ids,
    out_count,
):
    shape = jax.ShapeDtypeStruct
    counts = jnp.concatenate([in_ids, in_count, out_ids, out_count], axis=0)
    plan, copies = call(
        plan_kernel,
        (shape((8, 128), jnp.int32), shape((EXPERTS, 8, 128), jnp.int32)),
        [VMEM],
        (VMEM, VMEM),
    )(counts)
    plans = exchange(copies, "expert")
    which = jnp.max(plans[:, BRANCH_AT, 0])
    place = jnp.stack([lax.axis_index("x"), lax.axis_index("z")]).astype(jnp.int32)
    ids = expert_ids.T
    rows = probs.T
    plan, *three = lax.optimization_barrier((plan, gate_tiles, up_tiles, down_tiles))
    own = jnp.concatenate([tile[0] for tile in three], axis=0)
    sources = [own] + [moved(own, "x", shift) for shift in range(1, NX)]
    token_grad, prob_grad, gate, up, down = lax.switch(
        which,
        [functools.partial(rest, size) for size in SIZES],
        plan,
        plans,
        place,
        ids,
        rows,
        tokens,
        cotangent,
        *sources,
    )
    return token_grad, prob_grad.T, gate, up, down


def solution(mesh):
    finer = Mesh(mesh.devices.reshape(EXPERTS, NX, NZ), ("expert", "x", "z"))
    rows = P(("expert", "x", "z"), None)
    tiles = P("expert", ("x", "z"), None, None)
    table = P("expert", None)
    return jax.shard_map(
        local,
        mesh=finer,
        in_specs=(rows, rows, rows, rows, tiles, tiles, tiles, table, table, table, table),
        out_specs=(rows, rows, tiles, tiles, tiles),
        check_vma=False,
    )
```

```python
import functools

import jax
import jax.numpy as jnp
from jax import lax
from jax.experimental import pallas as pl
from jax.experimental.pallas import tpu as pltpu
from jax.sharding import Mesh
from jax.sharding import PartitionSpec as P

FF = 8192
TILE = 128
COL_BLOCKS = FF // TILE
EXPERTS = 8
NX = 4
NZ = 8
SLOTS = NX * NZ
CAP = 40
ROWS = 128
WIDTH = 3072
TOTAL = EXPERTS * CAP
PEERS = EXPERTS * NX
AHEAD = 16
IN_AT, OUT_AT, Z_AT, COUNT_AT, RANK_AT, BRANCH_AT = range(6)
SIZES = (3, 4, 8)
SENT = (1, 4, 7, 5, 2)
KEPT = (0, 3, 6)
WAVES = ((0, 2), (2, 2), (4, 1))

BF = jnp.bfloat16
F32 = jnp.float32
SMEM = pl.BlockSpec(memory_space=pltpu.SMEM)
VMEM = pl.BlockSpec(memory_space=pltpu.VMEM)
HBM = pl.BlockSpec(memory_space=pltpu.HBM)
LIMIT = 40 * 1024 * 1024


def call(kernel, out, ins, outs, scratch=(), cost=None):
    return pl.pallas_call(
        kernel,
        out_shape=out,
        in_specs=ins,
        out_specs=outs,
        scratch_shapes=list(scratch),
        cost_estimate=cost,
        compiler_params=pltpu.CompilerParams(vmem_limit_bytes=LIMIT),
    )


def dot(a, b):
    return lax.dot_general(a, b, (((1,), (0,)), ((), ())), preferred_element_type=F32)


def dot_nt(a, b):
    return lax.dot_general(a, b, (((1,), (1,)), ((), ())), preferred_element_type=F32)


def dot_tn(a, b):
    return lax.dot_general(a, b, (((0,), (0,)), ((), ())), preferred_element_type=F32)


def lean(per):
    return per > 4


def block(j, size):
    if isinstance(j, int):
        return slice(j * size, (j + 1) * size)
    return pl.ds(pl.multiple_of(j * size, size), size)


def each(count, body, per):
    if lean(per):
        lax.fori_loop(0, count, lambda j, _: body(j) or 0, 0)
    else:
        for j in range(count):
            body(j)


def back_tail(per):
    return 16 if per % 2 == 0 else 8


def plan_kernel(counts, plan, copies):
    slot_i = lax.broadcasted_iota(jnp.int32, (SLOTS, SLOTS), 0)
    slot_j = lax.broadcasted_iota(jnp.int32, (SLOTS, SLOTS), 1)
    order_i = (slot_i & (NZ - 1)) * NX + (slot_i >> 3)
    order_j = (slot_j & (NZ - 1)) * NX + (slot_j >> 3)

    def column(line):
        return jnp.sum(jnp.where(slot_i == slot_j, line, 0.0), axis=1, keepdims=True)

    live = jnp.logical_and(counts[1:2, :] > 0, counts[3:4, :] > 0).astype(F32)
    rank = jnp.sum(jnp.where(order_j < order_i, live, 0.0), axis=1, keepdims=True)
    live_column = column(live)
    hot = jnp.logical_and(rank == slot_j.astype(F32), live_column > 0.0)

    def by_rank(values):
        return jnp.sum(jnp.where(hot, values, 0.0), axis=0, keepdims=True)

    rank_line = jnp.sum(jnp.where(order_i < order_j, live_column, 0.0), axis=0, keepdims=True)
    count = jnp.sum(live, axis=1, keepdims=True) + jnp.zeros_like(live)
    branch = jnp.zeros_like(live)
    for size in SIZES[:-1]:
        branch = branch + (count > NX * size).astype(F32)
    plan[...] = jnp.zeros_like(plan)
    for at, line in (
        (IN_AT, by_rank(column((counts[0:1, :] >> 6).astype(F32)))),
        (OUT_AT, by_rank(column(counts[2:3, :].astype(F32)))),
        (Z_AT, by_rank((slot_i & (NZ - 1)).astype(F32))),
        (COUNT_AT, count),
        (RANK_AT, jnp.where(live > 0.0, rank_line, -1.0)),
        (BRANCH_AT, branch),
    ):
        plan[at : at + 1, :SLOTS] = line.astype(jnp.int32)
    whole = plan[...]
    for e in range(EXPERTS):
        copies[e] = whole


def assignment(ids):
    experts = lax.broadcasted_iota(jnp.int32, (EXPERTS, ROWS), 0)
    first = ids[0:1, :] == experts
    second = ids[1:2, :] == experts
    named = jnp.logical_or(first, second)
    above = lax.broadcasted_iota(jnp.int32, (ROWS, ROWS), 0) < lax.broadcasted_iota(
        jnp.int32, (ROWS, ROWS), 1
    )
    place = dot(named.astype(F32).astype(BF), above.astype(F32).astype(BF))
    return first, second, jnp.where(named, place, -1.0)


def one_hot(place):
    at = lax.broadcasted_iota(jnp.int32, (CAP, ROWS), 0).astype(F32)
    rows = [(place[e : e + 1, :] == at).astype(F32) for e in range(EXPERTS)]
    return jnp.concatenate(rows, axis=0).astype(BF)


def dispatch_kernel(per, plans, ids, probs, tokens, cot, sent, xs, ys, prob_rows, places, out, sem):
    first, second, place = assignment(ids[...])
    p = probs[...].astype(F32)
    prob_rows[...] = jnp.where(first, p[0:1, :], 0.0) + jnp.where(second, p[1:2, :], 0.0)
    places[...] = place
    pick = one_hot(place)

    def gather(j):
        at = block(j, 256)
        xs[:, at] = dot(pick, tokens[:, at])
        ys[:, at] = dot(pick, cot[:, at])

    each(WIDTH // 256, gather, per)
    line = lax.broadcasted_iota(jnp.int32, (AHEAD, ROWS), 0)

    def per_expert(e, _):
        rows = pl.ds(pl.multiple_of(e * CAP, 8), CAP)
        extra = jnp.where(
            line == 0,
            prob_rows[pl.ds(e, 1), :],
            jnp.where(line == 1, places[pl.ds(e, 1), :], 0.0),
        ).astype(BF)
        for x in range(NX):
            for k in range(per):
                r = k * NX + x
                at_in = pl.multiple_of(plans[e, IN_AT, r] * TILE, TILE)
                at_out = pl.multiple_of(plans[e, OUT_AT, r] * TILE, TILE)
                both = jnp.concatenate(
                    [xs[rows, pl.ds(at_in, TILE)], ys[rows, pl.ds(at_out, TILE)]], axis=0
                )
                out[e * NX + x, 2 * CAP * k : 2 * CAP * (k + 1), :] = both.astype(BF)
            out[e * NX + x, 2 * CAP * per : 2 * CAP * per + AHEAD, :] = extra
        leave(e).start()
        return 0

    def leave(e):
        part = pl.ds(e * NX, NX)
        return pltpu.make_async_copy(out.at[part], sent.at[part], sem.at[e])

    def wait(e, _):
        leave(e).wait()
        return 0

    lax.fori_loop(0, EXPERTS, per_expert, 0)
    lax.fori_loop(0, EXPERTS, wait, 0)


def pick_weights_kernel(plan, place, own, one, two, three, out):
    x, z = place[0], place[1]
    out[...] = jnp.zeros_like(out)
    for shift, source in enumerate((own, one, two, three)):
        home = lax.rem(x + NX - shift, NX)
        rank = plan[RANK_AT, home * NZ + z]

        @pl.when(jnp.logical_and(rank >= 0, lax.rem(rank + NX, NX) == x))
        def _():
            out[...] = source[...]


def pick_grads_kernel(plan, place, own, one, two, three, gate, up, down):
    x, z = place[0], place[1]
    rank = plan[RANK_AT, x * NZ + z]
    outs = (gate, up, down)
    for ref in outs:
        ref[...] = jnp.zeros_like(ref)
    for shift, source in enumerate((own, one, two, three)):
        home = lax.rem(x + NX - shift, NX)

        @pl.when(jnp.logical_and(rank >= 0, lax.rem(rank + NX, NX) == home))
        def _():
            for i, ref in enumerate(outs):
                ref[0, 0] = source[i].astype(F32)


def expert_kernel(per, plan, place, got, weights, sent, *refs):
    outs, refs = refs[: len(WAVES) + 1], refs[len(WAVES) + 1 :]
    pair, down, pair_sum, down_sum, back, kept, away, back_sem, grad_sem = refs
    x, own_z = place[0], place[1]
    count = plan[COUNT_AT, 0]
    for k in range(per):
        z = plan[Z_AT, k * NX + x]
        live = jnp.where(k * NX + x < count, 1.0, 0.0).astype(F32)
        for i in range(2):
            tile = weights[3 * z + i].astype(F32) * live
            pair[k, :, i * TILE : (i + 1) * TILE] = tile.astype(BF)
        down[k] = (weights[3 * z + 2].astype(F32) * live).astype(BF)
    pair_sum[...] = jnp.zeros_like(pair_sum)
    down_sum[...] = jnp.zeros_like(down_sum)
    group = 8
    rows = group * CAP
    tail = back_tail(per)
    ones = jnp.ones((ROWS, TILE), BF)

    def chunk(c, _):
        at = pl.ds(c * group, group)
        extra = got[at, 2 * CAP * per : 2 * CAP * per + AHEAD, :].astype(F32)
        slot = lax.broadcasted_iota(jnp.int32, (group, CAP, ROWS), 1).astype(F32)
        mine = extra[:, 1:2, :] == slot
        p = dot(jnp.where(mine, extra[:, 0:1, :], 0.0).reshape(rows, ROWS).astype(BF), ones)
        inner = jnp.zeros((rows, TILE), F32)
        pieces = []
        for k in range(per):
            both = got[at, 2 * CAP * k : 2 * CAP * (k + 1), :].astype(F32)
            rows_x = both[:, :CAP, :].reshape(rows, TILE).astype(BF)
            rows_dy = both[:, CAP:, :].reshape(rows, TILE)
            gu = dot(rows_x, pair[k])
            g, u = gu[:, :TILE], gu[:, TILE:]
            m = dot_nt(rows_dy.astype(BF), down[k])
            sig = jax.nn.sigmoid(g)
            act = g * sig
            h = (act * u).astype(BF)
            inner = inner + h.astype(F32) * m
            dh = p * m
            dg = (dh * u * sig * (1.0 + g * (1.0 - sig))).astype(BF)
            du = (dh * act).astype(BF)
            q = (p * rows_dy).astype(BF)
            dgu = jnp.concatenate([dg, du], axis=1)
            pieces.append(dot_nt(dgu, pair[k]).reshape(group, CAP, TILE))
            pair_sum[k] += dot_tn(rows_x, dgu)
            down_sum[k] += dot_tn(h, q)
        column = jnp.sum(inner, axis=1, keepdims=True).reshape(group, CAP, 1)
        row = jnp.sum(jnp.where(mine, column, 0.0), axis=1, keepdims=True)
        high = row.astype(BF).astype(F32)
        line = lax.broadcasted_iota(jnp.int32, (group, tail, ROWS), 1)
        pieces.append(jnp.where(line == 0, high, jnp.where(line == 1, row - high, 0.0)))
        back[at] = jnp.concatenate(pieces, axis=1).astype(BF)
        leave(c).start()
        return 0

    def leave(c):
        at = pl.ds(c * group, group)
        return pltpu.make_async_copy(back.at[at], sent.at[at], back_sem.at[c])

    def wait(c, _):
        leave(c).wait()
        return 0

    lax.fori_loop(0, PEERS // group, chunk, 0)
    kept[...] = jnp.zeros_like(kept)
    away[...] = jnp.zeros_like(away)
    for k in range(per):
        valid = k * NX + x < count
        shift = (plan[Z_AT, k * NX + x] - own_z) & (NZ - 1)

        for held, chunks in ((away, SENT), (kept, KEPT)):
            at = sum(jnp.where(shift == s, i, 0) for i, s in enumerate(chunks))
            known = functools.reduce(jnp.logical_or, [shift == s for s in chunks])

            @pl.when(jnp.logical_and(valid, known))
            def _():
                held[at, 0] = pair_sum[k, :, :TILE].astype(held.dtype)
                held[at, 1] = pair_sum[k, :, TILE:].astype(held.dtype)
                held[at, 2] = down_sum[k].astype(held.dtype)

    copies = [pltpu.make_async_copy(kept, outs[0], grad_sem.at[0])]
    for i, (start, size) in enumerate(WAVES):
        part = away.at[start : start + size]
        copies.append(pltpu.make_async_copy(part, outs[i + 1], grad_sem.at[i + 1]))
    for copy in copies:
        copy.start()
    for copy in copies:
        copy.wait()
    lax.fori_loop(0, PEERS // group, wait, 0)


def relay_kernel(kept, below, above, up, down, own):
    up[...] = (kept[1] + below[1].astype(F32)).astype(BF)
    down[...] = (kept[2] + above[1].astype(F32)).astype(BF)
    own[...] = kept[0] + below[0].astype(F32) + above[0].astype(F32)


def sum_kernel(own, two, up, down, whole, sent):
    total = own[...] + two[0].astype(F32) + up[...].astype(F32) + down[...].astype(F32)
    whole[...] = total
    sent[...] = total.astype(BF)


def combine_kernel(per, plans, ids, back, token_grad, prob_grad, parts, prob_rows):
    tail = back_tail(per)
    parts[...] = jnp.zeros_like(parts)

    def per_expert(e, _):
        rows = pl.ds(pl.multiple_of(e * CAP, 8), CAP)
        total = jnp.zeros((1, ROWS), F32)
        for x in range(NX):
            chunk = back[e * NX + x].astype(F32)
            for k in range(per):
                at = pl.multiple_of(plans[e, IN_AT, k * NX + x] * TILE, TILE)
                parts[rows, pl.ds(at, TILE)] += chunk[CAP * k : CAP * (k + 1), :]
            total = total + chunk[CAP * per : CAP * per + 1] + chunk[CAP * per + 1 : CAP * per + 2]
        prob_rows[pl.ds(e, 1), :] = total
        return 0

    lax.fori_loop(0, EXPERTS, per_expert, 0)
    first, second, place = assignment(ids[...])
    pick = one_hot(place)

    def gather(j):
        at = block(j, 256)
        token_grad[:, at] = dot_tn(pick, parts[:, at].astype(BF)).astype(BF)

    each(WIDTH // 256, gather, per)
    rows = prob_rows[...]
    prob_grad[...] = jnp.concatenate(
        [
            jnp.sum(jnp.where(first, rows, 0.0), axis=0, keepdims=True),
            jnp.sum(jnp.where(second, rows, 0.0), axis=0, keepdims=True),
        ],
        axis=0,
    ).astype(BF)


def exchange(values, axes):
    return lax.all_to_all(values, axes, split_axis=0, concat_axis=0, tiled=True)


def moved(values, axis, shift):
    size = lax.axis_size(axis)
    return lax.ppermute(values, axis, [(i, (i + shift) % size) for i in range(size)])


def rest(per, plan, plans, place, ids, probs, tokens, cotangent, weights):
    shape = jax.ShapeDtypeStruct
    triple = (3, TILE, TILE)
    ahead = 2 * CAP * per + AHEAD
    behind = CAP * per + back_tail(per)
    sent = call(
        functools.partial(dispatch_kernel, per),
        pltpu.HBM((PEERS, ahead, TILE), BF),
        [SMEM, VMEM, VMEM, VMEM, VMEM],
        HBM,
        [
            pltpu.VMEM((TOTAL, WIDTH), F32),
            pltpu.VMEM((TOTAL, WIDTH), F32),
            pltpu.VMEM((EXPERTS, ROWS), F32),
            pltpu.VMEM((EXPERTS, ROWS), F32),
            pltpu.VMEM((PEERS, ahead, TILE), BF),
            pltpu.SemaphoreType.DMA((EXPERTS,)),
        ],
    )(plans, ids, probs, tokens, cotangent)
    got = exchange(sent, ("expert", "x"))
    weights = lax.all_gather(weights, "z", axis=0, tiled=True)
    back, *grads = call(
        functools.partial(expert_kernel, per),
        (
            pltpu.HBM((PEERS, behind, TILE), BF),
            pltpu.HBM((3,) + triple, F32),
            *[pltpu.HBM((size,) + triple, BF) for _, size in WAVES],
        ),
        [SMEM, SMEM, VMEM, VMEM],
        [HBM] * (len(WAVES) + 2),
        [
            pltpu.VMEM((per, TILE, 2 * TILE), BF),
            pltpu.VMEM((per, TILE, TILE), BF),
            pltpu.VMEM((per, TILE, 2 * TILE), F32),
            pltpu.VMEM((per, TILE, TILE), F32),
            pltpu.VMEM((PEERS, behind, TILE), BF),
            pltpu.VMEM((3,) + triple, F32),
            pltpu.VMEM((5,) + triple, BF),
            pltpu.SemaphoreType.DMA((PEERS // 8,)),
            pltpu.SemaphoreType.DMA((len(WAVES) + 1,)),
        ],
    )(plan, place, got, weights)
    returned = exchange(back, ("expert", "x"))
    if lean(per):
        chunks = jnp.concatenate([grads[0], *[part.astype(F32) for part in grads[1:]]], axis=0)
        chunks = [chunks[(KEPT + SENT).index(shift)] for shift in range(NZ)]
        ordered = jnp.roll(jnp.stack(chunks), place[1], axis=0)
        own = jnp.sum(exchange(ordered, "z"), axis=0)
        whole = exchange(jnp.broadcast_to(own[None], (NX,) + triple), "x")
        nearby = [
            lax.dynamic_index_in_dim(whole, (place[0] + NX - shift) % NX, keepdims=False)
            for shift in range(1, NX)
        ]
    else:
        kept, plus_one, minus_one, plus_two = grads
        below, above = moved(plus_one, "z", 1), moved(minus_one, "z", NZ - 1)
        two = moved(plus_two, "z", 2)
        up, down, own = call(
            relay_kernel,
            (shape(triple, BF), shape(triple, BF), shape(triple, F32)),
            [VMEM] * 3,
            (VMEM,) * 3,
        )(kept, below, above)
        own, sent = call(
            sum_kernel, (shape(triple, F32), shape(triple, BF)), [VMEM] * 4, (VMEM, VMEM)
        )(own, two, moved(up, "z", 3), moved(down, "z", NZ - 2))
        nearby = [moved(sent, "x", shift) for shift in range(1, NX)]
    token_grad, prob_grad = call(
        functools.partial(combine_kernel, per),
        (shape((ROWS, WIDTH), BF), shape((2, ROWS), BF)),
        [SMEM, VMEM, VMEM],
        (VMEM, VMEM),
        [pltpu.VMEM((TOTAL, WIDTH), F32), pltpu.VMEM((EXPERTS, ROWS), F32)],
        pl.CostEstimate(
            flops=2 * ROWS * TOTAL * WIDTH,
            bytes_accessed=3 * 4 * TOTAL * WIDTH + 2 * PEERS * behind * TILE,
            transcendentals=0,
        ),
    )(plans, ids, returned)
    token_grad, *nearby = lax.optimization_barrier((token_grad, *nearby))
    tile = shape((1, 1, TILE, TILE), F32)
    gate, up, down = call(
        pick_grads_kernel,
        (tile, tile, tile),
        [SMEM, SMEM, VMEM, VMEM, VMEM, VMEM],
        (VMEM, VMEM, VMEM),
    )(plan, place, own, *nearby)
    return token_grad, prob_grad, gate, up, down


def local(
    tokens,
    cotangent,
    expert_ids,
    probs,
    gate_tiles,
    up_tiles,
    down_tiles,
    in_ids,
    in_count,
    out_ids,
    out_count,
):
    shape = jax.ShapeDtypeStruct
    counts = jnp.concatenate([in_ids, in_count, out_ids, out_count], axis=0)
    plan, copies = call(
        plan_kernel,
        (shape((8, 128), jnp.int32), shape((EXPERTS, 8, 128), jnp.int32)),
        [VMEM],
        (VMEM, VMEM),
    )(counts)
    plans = exchange(copies, "expert")
    place = jnp.stack([lax.axis_index("x"), lax.axis_index("z")]).astype(jnp.int32)
    ids = expert_ids.T
    rows = probs.T
    plan, *three = lax.optimization_barrier((plan, gate_tiles, up_tiles, down_tiles))
    own = jnp.concatenate([tile[0] for tile in three], axis=0)
    weights = call(
        pick_weights_kernel,
        shape((3, TILE, TILE), BF),
        [SMEM, SMEM, VMEM, VMEM, VMEM, VMEM],
        VMEM,
    )(plan, place, own, *[moved(own, "x", shift) for shift in range(1, NX)])
    plans, weights = lax.optimization_barrier((plans, weights))
    which = jnp.max(plans[:, BRANCH_AT, 0])
    token_grad, prob_grad, gate, up, down = lax.switch(
        which,
        [functools.partial(rest, size) for size in SIZES],
        plan,
        plans,
        place,
        ids,
        rows,
        tokens,
        cotangent,
        weights,
    )
    return token_grad, prob_grad.T, gate, up, down


def solution(mesh):
    finer = Mesh(mesh.devices.reshape(EXPERTS, NX, NZ), ("expert", "x", "z"))
    rows = P(("expert", "x", "z"), None)
    tiles = P("expert", ("x", "z"), None, None)
    table = P("expert", None)
    return jax.shard_map(
        local,
        mesh=finer,
        in_specs=(rows, rows, rows, rows, tiles, tiles, tiles, table, table, table, table),
        out_specs=(rows, rows, tiles, tiles, tiles),
        check_vma=False,
    )
```

```python
import functools

import jax
import jax.numpy as jnp
from jax import lax
from jax.experimental import pallas as pl
from jax.experimental.pallas import tpu as pltpu
from jax.sharding import Mesh
from jax.sharding import PartitionSpec as P

FF = 8192
TILE = 128
COL_BLOCKS = FF // TILE
EXPERTS = 8
NX = 4
NZ = 8
SLOTS = NX * NZ
CAP = 40
ROWS = 128
WIDTH = 3072
TOTAL = EXPERTS * CAP
PEERS = EXPERTS * NX
AHEAD = 16
IN_AT, OUT_AT, Z_AT, COUNT_AT, RANK_AT, BRANCH_AT = range(6)
SIZES = (3, 4, 8)
SENT = (1, 4, 7, 5, 2)
KEPT = (0, 3, 6)
WAVES = ((0, 2), (2, 2), (4, 1))

BF = jnp.bfloat16
F32 = jnp.float32
SMEM = pl.BlockSpec(memory_space=pltpu.SMEM)
VMEM = pl.BlockSpec(memory_space=pltpu.VMEM)
HBM = pl.BlockSpec(memory_space=pltpu.HBM)
LIMIT = 40 * 1024 * 1024


def call(kernel, out, ins, outs, scratch=(), cost=None):
    return pl.pallas_call(
        kernel,
        out_shape=out,
        in_specs=ins,
        out_specs=outs,
        scratch_shapes=list(scratch),
        cost_estimate=cost,
        compiler_params=pltpu.CompilerParams(vmem_limit_bytes=LIMIT),
    )


def dot(a, b):
    return lax.dot_general(a, b, (((1,), (0,)), ((), ())), preferred_element_type=F32)


def dot_nt(a, b):
    return lax.dot_general(a, b, (((1,), (1,)), ((), ())), preferred_element_type=F32)


def dot_tn(a, b):
    return lax.dot_general(a, b, (((0,), (0,)), ((), ())), preferred_element_type=F32)


def lean(per):
    return per > 4


def block(j, size):
    if isinstance(j, int):
        return slice(j * size, (j + 1) * size)
    return pl.ds(pl.multiple_of(j * size, size), size)


def each(count, body, per):
    if lean(per):
        lax.fori_loop(0, count, lambda j, _: body(j) or 0, 0)
    else:
        for j in range(count):
            body(j)


def back_tail(per):
    return 16 if per % 2 == 0 else 8


def plan_kernel(counts, plan, copies):
    slot_i = lax.broadcasted_iota(jnp.int32, (SLOTS, SLOTS), 0)
    slot_j = lax.broadcasted_iota(jnp.int32, (SLOTS, SLOTS), 1)
    order_i = (slot_i & (NZ - 1)) * NX + (slot_i >> 3)
    order_j = (slot_j & (NZ - 1)) * NX + (slot_j >> 3)

    def column(line):
        return jnp.sum(jnp.where(slot_i == slot_j, line, 0.0), axis=1, keepdims=True)

    live = jnp.logical_and(counts[1:2, :] > 0, counts[3:4, :] > 0).astype(F32)
    rank = jnp.sum(jnp.where(order_j < order_i, live, 0.0), axis=1, keepdims=True)
    live_column = column(live)
    hot = jnp.logical_and(rank == slot_j.astype(F32), live_column > 0.0)

    def by_rank(values):
        return jnp.sum(jnp.where(hot, values, 0.0), axis=0, keepdims=True)

    rank_line = jnp.sum(jnp.where(order_i < order_j, live_column, 0.0), axis=0, keepdims=True)
    count = jnp.sum(live, axis=1, keepdims=True) + jnp.zeros_like(live)
    branch = jnp.zeros_like(live)
    for size in SIZES[:-1]:
        branch = branch + (count > NX * size).astype(F32)
    plan[...] = jnp.zeros_like(plan)
    for at, line in (
        (IN_AT, by_rank(column((counts[0:1, :] >> 6).astype(F32)))),
        (OUT_AT, by_rank(column(counts[2:3, :].astype(F32)))),
        (Z_AT, by_rank((slot_i & (NZ - 1)).astype(F32))),
        (COUNT_AT, count),
        (RANK_AT, jnp.where(live > 0.0, rank_line, -1.0)),
        (BRANCH_AT, branch),
    ):
        plan[at : at + 1, :SLOTS] = line.astype(jnp.int32)
    whole = plan[...]
    for e in range(EXPERTS):
        copies[e] = whole


def assignment(ids):
    experts = lax.broadcasted_iota(jnp.int32, (EXPERTS, ROWS), 0)
    first = ids[0:1, :] == experts
    second = ids[1:2, :] == experts
    named = jnp.logical_or(first, second)
    above = lax.broadcasted_iota(jnp.int32, (ROWS, ROWS), 0) < lax.broadcasted_iota(
        jnp.int32, (ROWS, ROWS), 1
    )
    place = dot(named.astype(F32).astype(BF), above.astype(F32).astype(BF))
    return first, second, jnp.where(named, place, -1.0)


def one_hot(place):
    at = lax.broadcasted_iota(jnp.int32, (CAP, ROWS), 0).astype(F32)
    rows = [(place[e : e + 1, :] == at).astype(F32) for e in range(EXPERTS)]
    return jnp.concatenate(rows, axis=0).astype(BF)


def dispatch_kernel(per, plans, ids, probs, tokens, cot, sent, xs, ys, prob_rows, places, out, sem):
    first, second, place = assignment(ids[...])
    p = probs[...].astype(F32)
    prob_rows[...] = jnp.where(first, p[0:1, :], 0.0) + jnp.where(second, p[1:2, :], 0.0)
    places[...] = place
    pick = one_hot(place)

    def gather(j):
        at = block(j, 256)
        xs[:, at] = dot(pick, tokens[:, at])
        ys[:, at] = dot(pick, cot[:, at])

    each(WIDTH // 256, gather, per)
    line = lax.broadcasted_iota(jnp.int32, (AHEAD, ROWS), 0)

    def per_expert(e, _):
        rows = pl.ds(pl.multiple_of(e * CAP, 8), CAP)
        extra = jnp.where(
            line == 0,
            prob_rows[pl.ds(e, 1), :],
            jnp.where(line == 1, places[pl.ds(e, 1), :], 0.0),
        ).astype(BF)
        for x in range(NX):
            for k in range(per):
                r = k * NX + x
                at_in = pl.multiple_of(plans[e, IN_AT, r] * TILE, TILE)
                at_out = pl.multiple_of(plans[e, OUT_AT, r] * TILE, TILE)
                both = jnp.concatenate(
                    [xs[rows, pl.ds(at_in, TILE)], ys[rows, pl.ds(at_out, TILE)]], axis=0
                )
                out[e * NX + x, 2 * CAP * k : 2 * CAP * (k + 1), :] = both.astype(BF)
            out[e * NX + x, 2 * CAP * per : 2 * CAP * per + AHEAD, :] = extra
        leave(e).start()
        return 0

    def leave(e):
        part = pl.ds(e * NX, NX)
        return pltpu.make_async_copy(out.at[part], sent.at[part], sem.at[e])

    def wait(e, _):
        leave(e).wait()
        return 0

    lax.fori_loop(0, EXPERTS, per_expert, 0)
    lax.fori_loop(0, EXPERTS, wait, 0)


def pick_weights_kernel(plan, place, own, one, two, three, out):
    x, z = place[0], place[1]
    out[...] = jnp.zeros_like(out)
    for shift, source in enumerate((own, one, two, three)):
        home = lax.rem(x + NX - shift, NX)
        rank = plan[RANK_AT, home * NZ + z]

        @pl.when(jnp.logical_and(rank >= 0, lax.rem(rank + NX, NX) == x))
        def _():
            out[...] = source[...]


def pick_grads_kernel(plan, place, own, one, two, three, gate, up, down):
    x, z = place[0], place[1]
    rank = plan[RANK_AT, x * NZ + z]
    outs = (gate, up, down)
    for ref in outs:
        ref[...] = jnp.zeros_like(ref)
    for shift, source in enumerate((own, one, two, three)):
        home = lax.rem(x + NX - shift, NX)

        @pl.when(jnp.logical_and(rank >= 0, lax.rem(rank + NX, NX) == home))
        def _():
            for i, ref in enumerate(outs):
                ref[0, 0] = source[i].astype(F32)


def expert_kernel(per, plan, place, got, weights, sent, *refs):
    outs, refs = refs[: len(WAVES) + 1], refs[len(WAVES) + 1 :]
    pair, down, pair_sum, down_sum, back, kept, away, back_sem, grad_sem = refs
    x, own_z = place[0], place[1]
    count = plan[COUNT_AT, 0]
    for k in range(per):
        z = plan[Z_AT, k * NX + x]
        z = z - (z & 1) + ((z + own_z) & 1)
        live = jnp.where(k * NX + x < count, 1.0, 0.0).astype(F32)
        for i in range(2):
            tile = weights[3 * z + i].astype(F32) * live
            pair[k, :, i * TILE : (i + 1) * TILE] = tile.astype(BF)
        down[k] = (weights[3 * z + 2].astype(F32) * live).astype(BF)
    pair_sum[...] = jnp.zeros_like(pair_sum)
    down_sum[...] = jnp.zeros_like(down_sum)
    group = 8
    rows = group * CAP
    tail = back_tail(per)
    ones = jnp.ones((ROWS, TILE), BF)

    def chunk(c, _):
        at = pl.ds(c * group, group)
        extra = got[at, 2 * CAP * per : 2 * CAP * per + AHEAD, :].astype(F32)
        slot = lax.broadcasted_iota(jnp.int32, (group, CAP, ROWS), 1).astype(F32)
        mine = extra[:, 1:2, :] == slot
        p = dot(jnp.where(mine, extra[:, 0:1, :], 0.0).reshape(rows, ROWS).astype(BF), ones)
        inner = jnp.zeros((rows, TILE), F32)
        pieces = []
        for k in range(per):
            both = got[at, 2 * CAP * k : 2 * CAP * (k + 1), :].astype(F32)
            rows_x = both[:, :CAP, :].reshape(rows, TILE).astype(BF)
            rows_dy = both[:, CAP:, :].reshape(rows, TILE)
            gu = dot(rows_x, pair[k])
            g, u = gu[:, :TILE], gu[:, TILE:]
            m = dot_nt(rows_dy.astype(BF), down[k])
            sig = jax.nn.sigmoid(g)
            act = g * sig
            h = (act * u).astype(BF)
            inner = inner + h.astype(F32) * m
            dh = p * m
            dg = (dh * u * sig * (1.0 + g * (1.0 - sig))).astype(BF)
            du = (dh * act).astype(BF)
            q = (p * rows_dy).astype(BF)
            dgu = jnp.concatenate([dg, du], axis=1)
            pieces.append(dot_nt(dgu, pair[k]).reshape(group, CAP, TILE))
            pair_sum[k] += dot_tn(rows_x, dgu)
            down_sum[k] += dot_tn(h, q)
        column = jnp.sum(inner, axis=1, keepdims=True).reshape(group, CAP, 1)
        row = jnp.sum(jnp.where(mine, column, 0.0), axis=1, keepdims=True)
        high = row.astype(BF).astype(F32)
        line = lax.broadcasted_iota(jnp.int32, (group, tail, ROWS), 1)
        pieces.append(jnp.where(line == 0, high, jnp.where(line == 1, row - high, 0.0)))
        back[at] = jnp.concatenate(pieces, axis=1).astype(BF)
        leave(c).start()
        return 0

    def leave(c):
        at = pl.ds(c * group, group)
        return pltpu.make_async_copy(back.at[at], sent.at[at], back_sem.at[c])

    def wait(c, _):
        leave(c).wait()
        return 0

    lax.fori_loop(0, PEERS // group, chunk, 0)
    kept[...] = jnp.zeros_like(kept)
    away[...] = jnp.zeros_like(away)
    for k in range(per):
        valid = k * NX + x < count
        shift = (plan[Z_AT, k * NX + x] - own_z) & (NZ - 1)

        for held, chunks in ((away, SENT), (kept, KEPT)):
            at = sum(jnp.where(shift == s, i, 0) for i, s in enumerate(chunks))
            known = functools.reduce(jnp.logical_or, [shift == s for s in chunks])

            @pl.when(jnp.logical_and(valid, known))
            def _():
                held[at, 0] = pair_sum[k, :, :TILE].astype(held.dtype)
                held[at, 1] = pair_sum[k, :, TILE:].astype(held.dtype)
                held[at, 2] = down_sum[k].astype(held.dtype)

    copies = [pltpu.make_async_copy(kept, outs[0], grad_sem.at[0])]
    for i, (start, size) in enumerate(WAVES):
        part = away.at[start : start + size]
        copies.append(pltpu.make_async_copy(part, outs[i + 1], grad_sem.at[i + 1]))
    for copy in copies:
        copy.start()
    for copy in copies:
        copy.wait()
    lax.fori_loop(0, PEERS // group, wait, 0)


def relay_kernel(kept, below, above, up, down, own):
    up[...] = (kept[1] + below[1].astype(F32)).astype(BF)
    down[...] = (kept[2] + above[1].astype(F32)).astype(BF)
    own[...] = kept[0] + below[0].astype(F32) + above[0].astype(F32)


def sum_kernel(own, two, up, down, whole, sent):
    total = own[...] + two[0].astype(F32) + up[...].astype(F32) + down[...].astype(F32)
    whole[...] = total
    sent[...] = total.astype(BF)


def combine_kernel(per, plans, ids, back, token_out, prob_out, parts, prob_rows, token_grad, prob_grad, sem):
    tail = back_tail(per)
    parts[...] = jnp.zeros_like(parts)

    def per_expert(e, _):
        rows = pl.ds(pl.multiple_of(e * CAP, 8), CAP)
        total = jnp.zeros((1, ROWS), F32)
        for x in range(NX):
            chunk = back[e * NX + x].astype(F32)
            for k in range(per):
                at = pl.multiple_of(plans[e, IN_AT, k * NX + x] * TILE, TILE)
                parts[rows, pl.ds(at, TILE)] += chunk[CAP * k : CAP * (k + 1), :]
            total = total + chunk[CAP * per : CAP * per + 1] + chunk[CAP * per + 1 : CAP * per + 2]
        prob_rows[pl.ds(e, 1), :] = total
        return 0

    lax.fori_loop(0, EXPERTS, per_expert, 0)
    first, second, place = assignment(ids[...])
    pick = one_hot(place)
    rows = prob_rows[...]
    prob_grad[...] = jnp.concatenate(
        [
            jnp.sum(jnp.where(first, rows, 0.0), axis=0, keepdims=True),
            jnp.sum(jnp.where(second, rows, 0.0), axis=0, keepdims=True),
        ],
        axis=0,
    ).astype(BF)
    prob_copy = pltpu.make_async_copy(prob_grad, prob_out, sem.at[WIDTH // 256])
    prob_copy.start()

    def leave(j):
        at = block(j, 256)
        return pltpu.make_async_copy(token_grad.at[:, at], token_out.at[:, at], sem.at[j])

    def gather(j):
        at = block(j, 256)
        token_grad[:, at] = dot_tn(pick, parts[:, at].astype(BF)).astype(BF)
        leave(j).start()

    each(WIDTH // 256, gather, per)
    each(WIDTH // 256, lambda j: leave(j).wait(), per)
    prob_copy.wait()


def exchange(values, axes):
    return lax.all_to_all(values, axes, split_axis=0, concat_axis=0, tiled=True)


def moved(values, axis, shift):
    size = lax.axis_size(axis)
    return lax.ppermute(values, axis, [(i, (i + shift) % size) for i in range(size)])


def rest(per, plan, plans, place, ids, probs, tokens, cotangent, weights):
    shape = jax.ShapeDtypeStruct
    triple = (3, TILE, TILE)
    ahead = 2 * CAP * per + AHEAD
    behind = CAP * per + back_tail(per)
    sent = call(
        functools.partial(dispatch_kernel, per),
        pltpu.HBM((PEERS, ahead, TILE), BF),
        [SMEM, VMEM, VMEM, VMEM, VMEM],
        HBM,
        [
            pltpu.VMEM((TOTAL, WIDTH), F32),
            pltpu.VMEM((TOTAL, WIDTH), F32),
            pltpu.VMEM((EXPERTS, ROWS), F32),
            pltpu.VMEM((EXPERTS, ROWS), F32),
            pltpu.VMEM((PEERS, ahead, TILE), BF),
            pltpu.SemaphoreType.DMA((EXPERTS,)),
        ],
    )(plans, ids, probs, tokens, cotangent)
    got = exchange(sent, ("expert", "x"))
    other = lax.ppermute(weights, "z", [(i, i ^ 1) for i in range(NZ)])
    weights = lax.all_gather(
        jnp.concatenate([weights, other], axis=0),
        "z",
        axis_index_groups=[[i + j for j in range(0, NZ, 2)] for i in range(2)],
        axis=0,
        tiled=True,
    )
    back, *grads = call(
        functools.partial(expert_kernel, per),
        (
            pltpu.HBM((PEERS, behind, TILE), BF),
            pltpu.HBM((3,) + triple, F32),
            *[pltpu.HBM((size,) + triple, BF) for _, size in WAVES],
        ),
        [SMEM, SMEM, VMEM, VMEM],
        [HBM] * (len(WAVES) + 2),
        [
            pltpu.VMEM((per, TILE, 2 * TILE), BF),
            pltpu.VMEM((per, TILE, TILE), BF),
            pltpu.VMEM((per, TILE, 2 * TILE), F32),
            pltpu.VMEM((per, TILE, TILE), F32),
            pltpu.VMEM((PEERS, behind, TILE), BF),
            pltpu.VMEM((3,) + triple, F32),
            pltpu.VMEM((5,) + triple, BF),
            pltpu.SemaphoreType.DMA((PEERS // 8,)),
            pltpu.SemaphoreType.DMA((len(WAVES) + 1,)),
        ],
    )(plan, place, got, weights)
    returned = exchange(back, ("expert", "x"))
    if lean(per):
        chunks = jnp.concatenate([grads[0], *[part.astype(F32) for part in grads[1:]]], axis=0)
        chunks = [chunks[(KEPT + SENT).index(shift)] for shift in range(NZ)]
        ordered = jnp.roll(jnp.stack(chunks), place[1], axis=0)
        own = jnp.sum(exchange(ordered, "z"), axis=0)
        whole = exchange(jnp.broadcast_to(own[None], (NX,) + triple), "x")
        nearby = [
            lax.dynamic_index_in_dim(whole, (place[0] + NX - shift) % NX, keepdims=False)
            for shift in range(1, NX)
        ]
    else:
        kept, plus_one, minus_one, plus_two = grads
        below, above = moved(plus_one, "z", 1), moved(minus_one, "z", NZ - 1)
        two = moved(plus_two, "z", 2)
        up, down, own = call(
            relay_kernel,
            (shape(triple, BF), shape(triple, BF), shape(triple, F32)),
            [VMEM] * 3,
            (VMEM,) * 3,
        )(kept, below, above)
        own, sent = call(
            sum_kernel, (shape(triple, F32), shape(triple, BF)), [VMEM] * 4, (VMEM, VMEM)
        )(own, two, moved(up, "z", 3), moved(down, "z", NZ - 2))
        nearby = [moved(sent, "x", shift) for shift in range(1, NX)]
    token_grad, prob_grad = call(
        functools.partial(combine_kernel, per),
        (pltpu.HBM((ROWS, WIDTH), BF), pltpu.HBM((2, ROWS), BF)),
        [SMEM, VMEM, VMEM],
        (HBM, HBM),
        [
            pltpu.VMEM((TOTAL, WIDTH), F32),
            pltpu.VMEM((EXPERTS, ROWS), F32),
            pltpu.VMEM((ROWS, WIDTH), BF),
            pltpu.VMEM((2, ROWS), BF),
            pltpu.SemaphoreType.DMA((WIDTH // 256 + 1,)),
        ],
        pl.CostEstimate(
            flops=2 * ROWS * TOTAL * WIDTH,
            bytes_accessed=3 * 4 * TOTAL * WIDTH + 2 * PEERS * behind * TILE,
            transcendentals=0,
        ),
    )(plans, ids, returned)
    token_grad, *nearby = lax.optimization_barrier((token_grad, *nearby))
    tile = shape((1, 1, TILE, TILE), F32)
    gate, up, down = call(
        pick_grads_kernel,
        (tile, tile, tile),
        [SMEM, SMEM, VMEM, VMEM, VMEM, VMEM],
        (VMEM, VMEM, VMEM),
    )(plan, place, own, *nearby)
    return token_grad, prob_grad, gate, up, down


def local(
    tokens,
    cotangent,
    expert_ids,
    probs,
    gate_tiles,
    up_tiles,
    down_tiles,
    in_ids,
    in_count,
    out_ids,
    out_count,
):
    shape = jax.ShapeDtypeStruct
    counts = jnp.concatenate([in_ids, in_count, out_ids, out_count], axis=0)
    plan, copies = call(
        plan_kernel,
        (shape((8, 128), jnp.int32), shape((EXPERTS, 8, 128), jnp.int32)),
        [VMEM],
        (VMEM, VMEM),
    )(counts)
    plans = exchange(copies, "expert")
    place = jnp.stack([lax.axis_index("x"), lax.axis_index("z")]).astype(jnp.int32)
    ids = expert_ids.T
    rows = probs.T
    plan, *three = lax.optimization_barrier((plan, gate_tiles, up_tiles, down_tiles))
    own = jnp.concatenate([tile[0] for tile in three], axis=0)
    weights = call(
        pick_weights_kernel,
        shape((3, TILE, TILE), BF),
        [SMEM, SMEM, VMEM, VMEM, VMEM, VMEM],
        VMEM,
    )(plan, place, own, *[moved(own, "x", shift) for shift in range(1, NX)])
    plans, weights = lax.optimization_barrier((plans, weights))
    which = jnp.max(plans[:, BRANCH_AT, 0])
    token_grad, prob_grad, gate, up, down = lax.switch(
        which,
        [functools.partial(rest, size) for size in SIZES],
        plan,
        plans,
        place,
        ids,
        rows,
        tokens,
        cotangent,
        weights,
    )
    return token_grad, prob_grad.T, gate, up, down


def solution(mesh):
    finer = Mesh(mesh.devices.reshape(EXPERTS, NX, NZ), ("expert", "x", "z"))
    rows = P(("expert", "x", "z"), None)
    tiles = P("expert", ("x", "z"), None, None)
    table = P("expert", None)
    return jax.shard_map(
        local,
        mesh=finer,
        in_specs=(rows, rows, rows, rows, tiles, tiles, tiles, table, table, table, table),
        out_specs=(rows, rows, tiles, tiles, tiles),
        check_vma=False,
    )
```

```python
import functools

import jax
import jax.numpy as jnp
from jax import lax
from jax.experimental import pallas as pl
from jax.experimental.pallas import tpu as pltpu
from jax.sharding import Mesh
from jax.sharding import PartitionSpec as P

FF = 8192
TILE = 128
COL_BLOCKS = FF // TILE
EXPERTS = 8
NX = 4
NZ = 8
SLOTS = NX * NZ
CAP = 40
ROWS = 128
WIDTH = 3072
TOTAL = EXPERTS * CAP
PEERS = EXPERTS * NX
AHEAD = 16
IN_AT, OUT_AT, Z_AT, COUNT_AT, RANK_AT, BRANCH_AT = range(6)
SIZES = (3, 4, 8)
SENT = (1, 4, 7, 5, 2)
KEPT = (0, 3, 6)
WAVES = ((0, 2), (2, 2), (4, 1))

BF = jnp.bfloat16
F32 = jnp.float32
SMEM = pl.BlockSpec(memory_space=pltpu.SMEM)
VMEM = pl.BlockSpec(memory_space=pltpu.VMEM)
HBM = pl.BlockSpec(memory_space=pltpu.HBM)
LIMIT = 40 * 1024 * 1024


def call(kernel, out, ins, outs, scratch=(), cost=None):
    return pl.pallas_call(
        kernel,
        out_shape=out,
        in_specs=ins,
        out_specs=outs,
        scratch_shapes=list(scratch),
        cost_estimate=cost,
        compiler_params=pltpu.CompilerParams(vmem_limit_bytes=LIMIT),
    )


def dot(a, b):
    return lax.dot_general(a, b, (((1,), (0,)), ((), ())), preferred_element_type=F32)


def dot_nt(a, b):
    return lax.dot_general(a, b, (((1,), (1,)), ((), ())), preferred_element_type=F32)


def dot_tn(a, b):
    return lax.dot_general(a, b, (((0,), (0,)), ((), ())), preferred_element_type=F32)


def lean(per):
    return per > 4


def block(j, size):
    if isinstance(j, int):
        return slice(j * size, (j + 1) * size)
    return pl.ds(pl.multiple_of(j * size, size), size)


def each(count, body, per):
    if lean(per):
        lax.fori_loop(0, count, lambda j, _: body(j) or 0, 0)
    else:
        for j in range(count):
            body(j)


def back_tail(per):
    return 16 if per % 2 == 0 else 8


def plan_kernel(counts, plan, copies):
    slot_i = lax.broadcasted_iota(jnp.int32, (SLOTS, SLOTS), 0)
    slot_j = lax.broadcasted_iota(jnp.int32, (SLOTS, SLOTS), 1)
    order_i = (slot_i & (NZ - 1)) * NX + (slot_i >> 3)
    order_j = (slot_j & (NZ - 1)) * NX + (slot_j >> 3)

    def column(line):
        return jnp.sum(jnp.where(slot_i == slot_j, line, 0.0), axis=1, keepdims=True)

    live = jnp.logical_and(counts[1:2, :] > 0, counts[3:4, :] > 0).astype(F32)
    rank = jnp.sum(jnp.where(order_j < order_i, live, 0.0), axis=1, keepdims=True)
    live_column = column(live)
    hot = jnp.logical_and(rank == slot_j.astype(F32), live_column > 0.0)

    def by_rank(values):
        return jnp.sum(jnp.where(hot, values, 0.0), axis=0, keepdims=True)

    rank_line = jnp.sum(jnp.where(order_i < order_j, live_column, 0.0), axis=0, keepdims=True)
    count = jnp.sum(live, axis=1, keepdims=True) + jnp.zeros_like(live)
    branch = jnp.zeros_like(live)
    for size in SIZES[:-1]:
        branch = branch + (count > NX * size).astype(F32)
    plan[...] = jnp.zeros_like(plan)
    for at, line in (
        (IN_AT, by_rank(column((counts[0:1, :] >> 6).astype(F32)))),
        (OUT_AT, by_rank(column(counts[2:3, :].astype(F32)))),
        (Z_AT, by_rank((slot_i & (NZ - 1)).astype(F32))),
        (COUNT_AT, count),
        (RANK_AT, jnp.where(live > 0.0, rank_line, -1.0)),
        (BRANCH_AT, branch),
    ):
        plan[at : at + 1, :SLOTS] = line.astype(jnp.int32)
    whole = plan[...]
    for e in range(EXPERTS):
        copies[e] = whole


def assignment(ids):
    experts = lax.broadcasted_iota(jnp.int32, (EXPERTS, ROWS), 0)
    first = ids[0:1, :] == experts
    second = ids[1:2, :] == experts
    named = jnp.logical_or(first, second)
    above = lax.broadcasted_iota(jnp.int32, (ROWS, ROWS), 0) < lax.broadcasted_iota(
        jnp.int32, (ROWS, ROWS), 1
    )
    place = dot(named.astype(F32).astype(BF), above.astype(F32).astype(BF))
    return first, second, jnp.where(named, place, -1.0)


def one_hot(place):
    at = lax.broadcasted_iota(jnp.int32, (CAP, ROWS), 0).astype(F32)
    rows = [(place[e : e + 1, :] == at).astype(F32) for e in range(EXPERTS)]
    return jnp.concatenate(rows, axis=0).astype(BF)


def dispatch_kernel(per, plans, ids, probs, tokens, cot, sent, xs, ys, prob_rows, places, out, sem):
    first, second, place = assignment(ids[...])
    p = probs[...].astype(F32)
    prob_rows[...] = jnp.where(first, p[0:1, :], 0.0) + jnp.where(second, p[1:2, :], 0.0)
    places[...] = place
    pick = one_hot(place)

    def gather(j):
        at = block(j, 256)
        xs[:, at] = dot(pick, tokens[:, at])
        ys[:, at] = dot(pick, cot[:, at])

    each(WIDTH // 256, gather, per)
    line = lax.broadcasted_iota(jnp.int32, (AHEAD, ROWS), 0)

    def per_expert(e, _):
        rows = pl.ds(pl.multiple_of(e * CAP, 8), CAP)
        extra = jnp.where(
            line == 0,
            prob_rows[pl.ds(e, 1), :],
            jnp.where(line == 1, places[pl.ds(e, 1), :], 0.0),
        ).astype(BF)
        for x in range(NX):
            for k in range(per):
                r = k * NX + x
                at_in = pl.multiple_of(plans[e, IN_AT, r] * TILE, TILE)
                at_out = pl.multiple_of(plans[e, OUT_AT, r] * TILE, TILE)
                both = jnp.concatenate(
                    [xs[rows, pl.ds(at_in, TILE)], ys[rows, pl.ds(at_out, TILE)]], axis=0
                )
                out[e * NX + x, 2 * CAP * k : 2 * CAP * (k + 1), :] = both.astype(BF)
            out[e * NX + x, 2 * CAP * per : 2 * CAP * per + AHEAD, :] = extra
        leave(e).start()
        return 0

    def leave(e):
        part = pl.ds(e * NX, NX)
        return pltpu.make_async_copy(out.at[part], sent.at[part], sem.at[e])

    def wait(e, _):
        leave(e).wait()
        return 0

    lax.fori_loop(0, EXPERTS, per_expert, 0)
    lax.fori_loop(0, EXPERTS, wait, 0)


def pick_weights_kernel(plan, place, own, one, two, three, out):
    x, z = place[0], place[1]
    out[...] = jnp.zeros_like(out)
    for shift, source in enumerate((own, one, two, three)):
        home = lax.rem(x + NX - shift, NX)
        rank = plan[RANK_AT, home * NZ + z]

        @pl.when(jnp.logical_and(rank >= 0, lax.rem(rank + NX, NX) == x))
        def _():
            out[...] = source[...]


def pick_grads_kernel(plan, place, own, one, two, three, gate, up, down):
    x, z = place[0], place[1]
    rank = plan[RANK_AT, x * NZ + z]
    outs = (gate, up, down)
    for ref in outs:
        ref[...] = jnp.zeros_like(ref)
    for shift, source in enumerate((own, one, two, three)):
        home = lax.rem(x + NX - shift, NX)

        @pl.when(jnp.logical_and(rank >= 0, lax.rem(rank + NX, NX) == home))
        def _():
            for i, ref in enumerate(outs):
                ref[0, 0] = source[i].astype(F32)


def expert_kernel(per, plan, place, got, weights, sent, *refs):
    outs, refs = refs[: len(WAVES) + 1], refs[len(WAVES) + 1 :]
    pair, down, pair_sum, down_sum, back, kept, away, back_sem, grad_sem = refs
    x, own_z = place[0], place[1]
    count = plan[COUNT_AT, 0]
    for k in range(per):
        z = plan[Z_AT, k * NX + x]
        z = z - (z & 1) + ((z + own_z) & 1)
        live = jnp.where(k * NX + x < count, 1.0, 0.0).astype(F32)
        for i in range(2):
            tile = weights[3 * z + i].astype(F32) * live
            pair[k, :, i * TILE : (i + 1) * TILE] = tile.astype(BF)
        down[k] = (weights[3 * z + 2].astype(F32) * live).astype(BF)
    pair_sum[...] = jnp.zeros_like(pair_sum)
    down_sum[...] = jnp.zeros_like(down_sum)
    group = 16
    rows = group * CAP
    tail = back_tail(per)
    ones = jnp.ones((ROWS, TILE), BF)

    def chunk(c, _):
        at = pl.ds(c * group, group)
        extra = got[at, 2 * CAP * per : 2 * CAP * per + AHEAD, :].astype(F32)
        slot = lax.broadcasted_iota(jnp.int32, (group, CAP, ROWS), 1).astype(F32)
        mine = extra[:, 1:2, :] == slot
        p = dot(jnp.where(mine, extra[:, 0:1, :], 0.0).reshape(rows, ROWS).astype(BF), ones)
        inner = jnp.zeros((rows, TILE), F32)
        pieces = []
        for k in range(per):
            both = got[at, 2 * CAP * k : 2 * CAP * (k + 1), :].astype(F32)
            rows_x = both[:, :CAP, :].reshape(rows, TILE).astype(BF)
            rows_dy = both[:, CAP:, :].reshape(rows, TILE)
            gu = dot(rows_x, pair[k])
            g, u = gu[:, :TILE], gu[:, TILE:]
            m = dot_nt(rows_dy.astype(BF), down[k])
            sig = jax.nn.sigmoid(g)
            act = g * sig
            h = (act * u).astype(BF)
            inner = inner + h.astype(F32) * m
            dh = p * m
            dg = (dh * u * sig * (1.0 + g * (1.0 - sig))).astype(BF)
            du = (dh * act).astype(BF)
            q = (p * rows_dy).astype(BF)
            dgu = jnp.concatenate([dg, du], axis=1)
            pieces.append(dot_nt(dgu, pair[k]).reshape(group, CAP, TILE))
            pair_sum[k] += dot_tn(rows_x, dgu)
            down_sum[k] += dot_tn(h, q)
        column = jnp.sum(inner, axis=1, keepdims=True).reshape(group, CAP, 1)
        row = jnp.sum(jnp.where(mine, column, 0.0), axis=1, keepdims=True)
        high = row.astype(BF).astype(F32)
        line = lax.broadcasted_iota(jnp.int32, (group, tail, ROWS), 1)
        pieces.append(jnp.where(line == 0, high, jnp.where(line == 1, row - high, 0.0)))
        back[at] = jnp.concatenate(pieces, axis=1).astype(BF)
        leave(c).start()
        return 0

    def leave(c):
        at = pl.ds(c * group, group)
        return pltpu.make_async_copy(back.at[at], sent.at[at], back_sem.at[c])

    def wait(c, _):
        leave(c).wait()
        return 0

    lax.fori_loop(0, PEERS // group, chunk, 0)
    kept[...] = jnp.zeros_like(kept)
    away[...] = jnp.zeros_like(away)
    for k in range(per):
        valid = k * NX + x < count
        shift = (plan[Z_AT, k * NX + x] - own_z) & (NZ - 1)

        for held, chunks in ((away, SENT), (kept, KEPT)):
            at = sum(jnp.where(shift == s, i, 0) for i, s in enumerate(chunks))
            known = functools.reduce(jnp.logical_or, [shift == s for s in chunks])

            @pl.when(jnp.logical_and(valid, known))
            def _():
                held[at, 0] = pair_sum[k, :, :TILE].astype(held.dtype)
                held[at, 1] = pair_sum[k, :, TILE:].astype(held.dtype)
                held[at, 2] = down_sum[k].astype(held.dtype)

    copies = [pltpu.make_async_copy(kept, outs[0], grad_sem.at[0])]
    for i, (start, size) in enumerate(WAVES):
        part = away.at[start : start + size]
        copies.append(pltpu.make_async_copy(part, outs[i + 1], grad_sem.at[i + 1]))
    for copy in copies:
        copy.start()
    for copy in copies:
        copy.wait()
    lax.fori_loop(0, PEERS // group, wait, 0)


def relay_kernel(kept, below, above, up, down, own):
    up[...] = (kept[1] + below[1].astype(F32)).astype(BF)
    down[...] = (kept[2] + above[1].astype(F32)).astype(BF)
    own[...] = kept[0] + below[0].astype(F32) + above[0].astype(F32)


def sum_kernel(own, two, up, down, whole, sent):
    total = own[...] + two[0].astype(F32) + up[...].astype(F32) + down[...].astype(F32)
    whole[...] = total
    sent[...] = total.astype(BF)


def combine_kernel(per, plans, ids, back, token_out, prob_out, parts, prob_rows, token_grad, prob_grad, sem):
    tail = back_tail(per)
    parts[...] = jnp.zeros_like(parts)

    def per_expert(e, _):
        rows = pl.ds(pl.multiple_of(e * CAP, 8), CAP)
        total = jnp.zeros((1, ROWS), F32)
        for x in range(NX):
            chunk = back[e * NX + x].astype(F32)
            for k in range(per):
                at = pl.multiple_of(plans[e, IN_AT, k * NX + x] * TILE, TILE)
                parts[rows, pl.ds(at, TILE)] += chunk[CAP * k : CAP * (k + 1), :]
            total = total + chunk[CAP * per : CAP * per + 1] + chunk[CAP * per + 1 : CAP * per + 2]
        prob_rows[pl.ds(e, 1), :] = total
        return 0

    lax.fori_loop(0, EXPERTS, per_expert, 0)
    first, second, place = assignment(ids[...])
    pick = one_hot(place)
    rows = prob_rows[...]
    prob_grad[...] = jnp.concatenate(
        [
            jnp.sum(jnp.where(first, rows, 0.0), axis=0, keepdims=True),
            jnp.sum(jnp.where(second, rows, 0.0), axis=0, keepdims=True),
        ],
        axis=0,
    ).astype(BF)
    prob_copy = pltpu.make_async_copy(prob_grad, prob_out, sem.at[WIDTH // 256])
    prob_copy.start()

    def leave(j):
        at = block(j, 256)
        return pltpu.make_async_copy(token_grad.at[:, at], token_out.at[:, at], sem.at[j])

    def gather(j):
        at = block(j, 256)
        token_grad[:, at] = dot_tn(pick, parts[:, at].astype(BF)).astype(BF)
        leave(j).start()

    each(WIDTH // 256, gather, per)
    each(WIDTH // 256, lambda j: leave(j).wait(), per)
    prob_copy.wait()


def exchange(values, axes):
    return lax.all_to_all(values, axes, split_axis=0, concat_axis=0, tiled=True)


def moved(values, axis, shift):
    size = lax.axis_size(axis)
    return lax.ppermute(values, axis, [(i, (i + shift) % size) for i in range(size)])


def rest(per, plan, plans, place, ids, probs, tokens, cotangent, weights):
    shape = jax.ShapeDtypeStruct
    triple = (3, TILE, TILE)
    ahead = 2 * CAP * per + AHEAD
    behind = CAP * per + back_tail(per)
    sent = call(
        functools.partial(dispatch_kernel, per),
        pltpu.HBM((PEERS, ahead, TILE), BF),
        [SMEM, VMEM, VMEM, VMEM, VMEM],
        HBM,
        [
            pltpu.VMEM((TOTAL, WIDTH), F32),
            pltpu.VMEM((TOTAL, WIDTH), F32),
            pltpu.VMEM((EXPERTS, ROWS), F32),
            pltpu.VMEM((EXPERTS, ROWS), F32),
            pltpu.VMEM((PEERS, ahead, TILE), BF),
            pltpu.SemaphoreType.DMA((EXPERTS,)),
        ],
    )(plans, ids, probs, tokens, cotangent)
    got = exchange(sent, ("expert", "x"))
    other = lax.ppermute(weights, "z", [(i, i ^ 1) for i in range(NZ)])
    weights = lax.all_gather(
        jnp.concatenate([weights, other], axis=0),
        "z",
        axis_index_groups=[[i + j for j in range(0, NZ, 2)] for i in range(2)],
        axis=0,
        tiled=True,
    )
    back, *grads = call(
        functools.partial(expert_kernel, per),
        (
            pltpu.HBM((PEERS, behind, TILE), BF),
            pltpu.HBM((3,) + triple, F32),
            *[pltpu.HBM((size,) + triple, BF) for _, size in WAVES],
        ),
        [SMEM, SMEM, VMEM, VMEM],
        [HBM] * (len(WAVES) + 2),
        [
            pltpu.VMEM((per, TILE, 2 * TILE), BF),
            pltpu.VMEM((per, TILE, TILE), BF),
            pltpu.VMEM((per, TILE, 2 * TILE), F32),
            pltpu.VMEM((per, TILE, TILE), F32),
            pltpu.VMEM((PEERS, behind, TILE), BF),
            pltpu.VMEM((3,) + triple, F32),
            pltpu.VMEM((5,) + triple, BF),
            pltpu.SemaphoreType.DMA((PEERS // 8,)),
            pltpu.SemaphoreType.DMA((len(WAVES) + 1,)),
        ],
    )(plan, place, got, weights)
    returned = exchange(back, ("expert", "x"))
    if lean(per):
        chunks = jnp.concatenate([grads[0], *[part.astype(F32) for part in grads[1:]]], axis=0)
        chunks = [chunks[(KEPT + SENT).index(shift)] for shift in range(NZ)]
        ordered = jnp.roll(jnp.stack(chunks), place[1], axis=0)
        own = jnp.sum(exchange(ordered, "z"), axis=0)
        whole = exchange(jnp.broadcast_to(own[None], (NX,) + triple), "x")
        nearby = [
            lax.dynamic_index_in_dim(whole, (place[0] + NX - shift) % NX, keepdims=False)
            for shift in range(1, NX)
        ]
    else:
        kept, plus_one, minus_one, plus_two = grads
        below, above = moved(plus_one, "z", 1), moved(minus_one, "z", NZ - 1)
        two = moved(plus_two, "z", 2)
        up, down, own = call(
            relay_kernel,
            (shape(triple, BF), shape(triple, BF), shape(triple, F32)),
            [VMEM] * 3,
            (VMEM,) * 3,
        )(kept, below, above)
        own, sent = call(
            sum_kernel, (shape(triple, F32), shape(triple, BF)), [VMEM] * 4, (VMEM, VMEM)
        )(own, two, moved(up, "z", 3), moved(down, "z", NZ - 2))
        nearby = [moved(sent, "x", shift) for shift in range(1, NX)]
    token_grad, prob_grad = call(
        functools.partial(combine_kernel, per),
        (pltpu.HBM((ROWS, WIDTH), BF), pltpu.HBM((2, ROWS), BF)),
        [SMEM, VMEM, VMEM],
        (HBM, HBM),
        [
            pltpu.VMEM((TOTAL, WIDTH), F32),
            pltpu.VMEM((EXPERTS, ROWS), F32),
            pltpu.VMEM((ROWS, WIDTH), BF),
            pltpu.VMEM((2, ROWS), BF),
            pltpu.SemaphoreType.DMA((WIDTH // 256 + 1,)),
        ],
        pl.CostEstimate(
            flops=2 * ROWS * TOTAL * WIDTH,
            bytes_accessed=3 * 4 * TOTAL * WIDTH + 2 * PEERS * behind * TILE,
            transcendentals=0,
        ),
    )(plans, ids, returned)
    token_grad, *nearby = lax.optimization_barrier((token_grad, *nearby))
    tile = shape((1, 1, TILE, TILE), F32)
    gate, up, down = call(
        pick_grads_kernel,
        (tile, tile, tile),
        [SMEM, SMEM, VMEM, VMEM, VMEM, VMEM],
        (VMEM, VMEM, VMEM),
    )(plan, place, own, *nearby)
    return token_grad, prob_grad, gate, up, down


def local(
    tokens,
    cotangent,
    expert_ids,
    probs,
    gate_tiles,
    up_tiles,
    down_tiles,
    in_ids,
    in_count,
    out_ids,
    out_count,
):
    shape = jax.ShapeDtypeStruct
    counts = jnp.concatenate([in_ids, in_count, out_ids, out_count], axis=0)
    plan, copies = call(
        plan_kernel,
        (shape((8, 128), jnp.int32), shape((EXPERTS, 8, 128), jnp.int32)),
        [VMEM],
        (VMEM, VMEM),
    )(counts)
    plans = exchange(copies, "expert")
    place = jnp.stack([lax.axis_index("x"), lax.axis_index("z")]).astype(jnp.int32)
    ids = expert_ids.T
    rows = probs.T
    plan, *three = lax.optimization_barrier((plan, gate_tiles, up_tiles, down_tiles))
    own = jnp.concatenate([tile[0] for tile in three], axis=0)
    weights = call(
        pick_weights_kernel,
        shape((3, TILE, TILE), BF),
        [SMEM, SMEM, VMEM, VMEM, VMEM, VMEM],
        VMEM,
    )(plan, place, own, *[moved(own, "x", shift) for shift in range(1, NX)])
    plans, weights = lax.optimization_barrier((plans, weights))
    which = jnp.max(plans[:, BRANCH_AT, 0])
    token_grad, prob_grad, gate, up, down = lax.switch(
        which,
        [functools.partial(rest, size) for size in SIZES],
        plan,
        plans,
        place,
        ids,
        rows,
        tokens,
        cotangent,
        weights,
    )
    return token_grad, prob_grad.T, gate, up, down


def solution(mesh):
    finer = Mesh(mesh.devices.reshape(EXPERTS, NX, NZ), ("expert", "x", "z"))
    rows = P(("expert", "x", "z"), None)
    tiles = P("expert", ("x", "z"), None, None)
    table = P("expert", None)
    return jax.shard_map(
        local,
        mesh=finer,
        in_specs=(rows, rows, rows, rows, tiles, tiles, tiles, table, table, table, table),
        out_specs=(rows, rows, tiles, tiles, tiles),
        check_vma=False,
    )
```
